256 devices in a mesh: lat: 16 (over x, y_lo, core), lon: 16 (over y_hi, z).
Axes of the slice: x: 4, y: 4 (y_hi: 2, y_lo: 2; y = y_hi * 2 + y_lo), z: 8, core: 2. Of those that a mesh axis runs over, the one named last changes fastest.
Arguments:
- fields: float32 [78, 32, 2048], P(None, 'lat', 'lon'), may hold values from -6 to 6
- diffusivity: float32 [32, 2048], P('lat', 'lon'), may hold values from 0.1 to 1.5
- w_embed: float32 [78, 256], replicated, may hold values from -0.625 to 0.625
- query_weight: float32 [256, 256], replicated, may hold values from -12 to 12
- key_weight: float32 [256, 256], replicated, may hold values from -1 to 1
- value_weight: float32 [256, 256], replicated, may hold values from -0.375 to 0.375
- out_weight: float32 [256, 256], replicated, may hold values from -0.375 to 0.375
- up_weight: float32 [256, 1024], replicated, may hold values from -0.375 to 0.375
- down_weight: float32 [1024, 256], replicated, may hold values from -0.1875 to 0.1875
Outputs:
- block_out: float32 [32, 2048, 256], P('lat', 'lon')
The draws below stay inside these ranges and needn't reach their ends.
All inputs are finite; a program needn't handle non-finite values.
Results may differ from the reference program's by a relative error of at most 0.0003.
Values sent between devices are 32-bit elements; how exact they have to be, the bound alone decides.
No kernel may reach another device: no remote copies, remote signals or barrier semaphores. Data moves between devices by JAX's collectives and lax.ppermute only.
A program may use at most 128 MiB of HBM per device.

```python
import math
import jax
import jax.numpy as jnp
from jax import lax

D = 256
HEADS = 8
FF = 1024
CHANNELS = 78
NLAT = 32
NLON = 2048


def shared_keys(key):
    raw = jax.random.normal(jax.random.fold_in(key, 11), (D, D), jnp.float32)
    return jnp.clip(raw, -6.0, 6.0) / math.sqrt(D)


def draw_key_weight(key, part):
    return shared_keys(key)


def draw_query_weight(key, part):
    fresh = jnp.clip(jax.random.normal(jax.random.fold_in(key, 23), (D, D), jnp.float32), -6.0, 6.0) / math.sqrt(D)
    return fresh


def levels(rng, dims, cuts, low, high):
    level = 1.0
    for position, parts in cuts:
        draws = jax.random.uniform(jax.random.fold_in(jax.random.fold_in(rng, 6), position), (parts,), jnp.float32, low / len(cuts), high / len(cuts))
        level = level * jnp.repeat(jnp.exp(draws), dims[position] // parts).reshape((-1,) + (1,) * (len(dims) - 1 - position))
    return level


def normal_values(rng, extent, spread, bound, pieces=(), kind=jnp.bfloat16):
    gain = levels(rng, extent, pieces, -0.22, 0.18) if pieces else 1.0
    entries = jax.random.normal(rng, extent, jnp.float32) * spread * gain
    return jnp.minimum(jnp.maximum(entries, -bound), bound).astype(kind)


def setup_inputs(seed: int = 0) -> dict:
    arg_keys = jax.random.split(jax.random.key(seed), 10)
    return {
        "fields": normal_values(arg_keys[0], (CHANNELS, NLAT, NLON), 1.0, 6.0, ((1, 16), (2, 16)), jnp.float32),
        "diffusivity": jnp.clip(jnp.exp(math.log(1.5) - 2.7080502 * jax.random.uniform(arg_keys[1], (NLAT, NLON), jnp.float32) ** levels(arg_keys[1], (NLAT, NLON), ((0, 16), (1, 16)), -0.2, 0.2)), 0.1, 1.5),
        "w_embed": normal_values(arg_keys[2], (CHANNELS, D), CHANNELS ** -0.5, 0.625, (), jnp.float32),
        "query_weight": draw_query_weight(jax.random.fold_in(arg_keys[9], 71), 0),
        "key_weight": draw_key_weight(jax.random.fold_in(arg_keys[9], 71), 0),
        "value_weight": normal_values(arg_keys[5], (D, D), D ** -0.5, 0.375, (), jnp.float32),
        "out_weight": normal_values(arg_keys[6], (D, D), D ** -0.5, 0.375, (), jnp.float32),
        "up_weight": normal_values(arg_keys[7], (D, FF), D ** -0.5, 0.375, (), jnp.float32),
        "down_weight": normal_values(arg_keys[8], (FF, D), FF ** -0.5, 0.1875, (), jnp.float32),
    }


HIGH = lax.Precision.HIGHEST
STEP_SIZE = 0.15
CENTER_LAT = 45.0
SPACING = 0.25
EPSILON = 1e-05

def cosines(first_row, count, total):
    faces = first_row.astype(jnp.float32) + jnp.arange(count + 1, dtype=jnp.float32)
    face_deg = CENTER_LAT + (faces - 0.5 * total) * SPACING
    cell_deg = CENTER_LAT + (faces[:-1] + 0.5 - 0.5 * total) * SPACING
    return (jnp.cos(face_deg * (math.pi / 180.0)), jnp.cos(cell_deg * (math.pi / 180.0)))

def tendency(padded_lat, padded_lon, face_cos, cell_cos):
    fields_lat = padded_lat[:-1]
    kappa_lat = padded_lat[-1]
    north_coef = 0.5 * (kappa_lat[1:] + kappa_lat[:-1]) * face_cos[:, None]
    north_flux = north_coef * (fields_lat[:, 1:] - fields_lat[:, :-1])
    lat_term = north_flux[:, 1:] - north_flux[:, :-1]
    fields_lon = padded_lon[:-1]
    kappa_lon = padded_lon[-1]
    east_coef = 0.5 * (kappa_lon[:, 1:] + kappa_lon[:, :-1])
    east_flux = east_coef * (fields_lon[:, :, 1:] - fields_lon[:, :, :-1])
    lon_term = (east_flux[:, :, 1:] - east_flux[:, :, :-1]) / cell_cos[:, None]
    return (lat_term + lon_term) / cell_cos[:, None]

def layer_norm(values):
    mean = lax.optimization_barrier(jnp.mean(values, axis=-1, keepdims=True))
    centered = values - mean
    variance = lax.optimization_barrier(jnp.mean(centered * centered, axis=-1, keepdims=True))
    return centered * lax.rsqrt(variance + EPSILON)

def project(values, weight):
    return jnp.einsum('yxd,de->yxe', values, weight, precision=HIGH)

def reference(fields, diffusivity, w_embed, query_weight, key_weight, value_weight, out_weight, up_weight, down_weight):
    channels, total_rows, total_lon = fields.shape
    stacked = jnp.concatenate([fields, diffusivity[None]], axis=0)
    padded_lat = jnp.pad(stacked, ((0, 0), (1, 1), (0, 0)))
    padded_lon = jnp.concatenate([stacked[:, :, -1:], stacked, stacked[:, :, :1]], axis=2)
    face_cos, cell_cos = cosines(jnp.int32(0), total_rows, total_rows)
    updated = fields + STEP_SIZE * tendency(padded_lat, padded_lon, face_cos, cell_cos)
    hidden = jnp.einsum('cyx,cd->yxd', updated, w_embed, precision=HIGH)
    normed = layer_norm(hidden)
    queries = project(normed, query_weight)
    key_rows = project(normed, key_weight)
    value_rows = project(normed, value_weight)
    width = hidden.shape[2]
    head_dim = width // HEADS
    scale = 1.0 / math.sqrt(head_dim)

    def one_circle(operands):
        query_row, key_row, value_row = operands
        query_heads = query_row.reshape(total_lon, HEADS, head_dim)
        key_heads = key_row.reshape(total_lon, HEADS, head_dim)
        value_heads = value_row.reshape(total_lon, HEADS, head_dim)
        scores = jnp.einsum('qhe,khe->hqk', query_heads, key_heads, precision=HIGH) * scale
        largest = lax.optimization_barrier(jnp.max(scores, axis=-1, keepdims=True))
        weights = jnp.exp(scores - largest)
        weights = weights / lax.optimization_barrier(jnp.sum(weights, axis=-1, keepdims=True))
        result = jnp.einsum('hqk,khe->qhe', weights, value_heads, precision=HIGH)
        return result.reshape(total_lon, width)
    attended = lax.map(one_circle, (queries, key_rows, value_rows))
    mixed = hidden + project(attended, out_weight)
    normed_two = layer_norm(mixed)
    activated = jax.nn.gelu(project(normed_two, up_weight))
    return mixed + project(activated, down_weight)
```

```python
import functools
import math

import jax
import jax.numpy as jnp
from jax import lax
from jax.experimental import pallas as pl
from jax.experimental.pallas import tpu as pltpu
from jax.sharding import PartitionSpec as P

HEADS = 8
STEP_SIZE = 0.15
CENTER_LAT = 45.0
SPACING = 0.25
EPSILON = 1e-05
ROWS = 80
F32 = jnp.float32
BF16 = jnp.bfloat16
VMEM = pl.BlockSpec(memory_space=pltpu.VMEM)
SMEM = pl.BlockSpec(memory_space=pltpu.SMEM)


def split(values):
    high = values.astype(BF16)
    return high, (values - high.astype(F32)).astype(BF16)


def dot(left, right):
    return jnp.dot(left, right, preferred_element_type=F32)


def dot3(left, right):
    return dot(left[0], right[0]) + dot(left[1], right[0]) + dot(left[0], right[1])


def pack_kernel(fields_ref, kappa_ref, both_ref, mine_ref, other_ref):
    y = lax.axis_index("lon") // 8
    channels = fields_ref.shape[0]
    zero = jnp.zeros((1, 128), F32)
    rows = []
    for row in range(2):
        rows.append(
            jnp.concatenate([fields_ref[:, row, :], kappa_ref[row : row + 1, :], zero], axis=0)
        )
    flag = (jnp.zeros((ROWS, 128), jnp.int32) + y) == 0
    mine = jnp.where(flag, rows[0], rows[1])
    other = jnp.where(flag, rows[1], rows[0])
    both_ref[0] = mine
    both_ref[1] = other
    mine_ref[...] = mine
    other_ref[...] = other


def stencil_kernel(cos_ref, both_ref, outer_ref, partner_ref, partner_outer_ref, chunk_ref):
    inverse = 1.0 / cos_ref[0]
    face_inner = cos_ref[1]
    face_outer = cos_ref[2]
    lane = lax.broadcasted_iota(jnp.int32, (ROWS, 128), 1)
    sectors = (
        (both_ref[0], both_ref[1], outer_ref[...]),
        (partner_ref[1], partner_ref[0], partner_outer_ref[...]),
    )
    for index, (q, inner, outer) in enumerate(sectors):
        kappa = q[78:79]
        lat_term = (0.5 * (kappa + inner[78:79]) * face_inner) * (inner - q)
        lat_term = lat_term + (0.5 * (kappa + outer[78:79]) * face_outer) * (outer - q)
        east = pltpu.roll(q, 127, 1)
        flux = (0.5 * (kappa + east[78:79])) * (east - q)
        flux = jnp.where(lane == 127, 0.0, flux)
        lon_term = flux - pltpu.roll(flux, 1, 1)
        updated = q + STEP_SIZE * ((lat_term + lon_term * inverse) * inverse)
        padded = jnp.concatenate([q, jnp.zeros((128 - ROWS, 128), F32)], axis=0)
        turned = jnp.transpose(padded)
        chunk_ref[index] = updated
        chunk_ref[index, 78:79, :] = turned[0:1]
        chunk_ref[index, 79:80, :] = turned[127:128]


def weights_kernel(
    embed_ref, query_ref, key_ref, value_ref, out_ref, up_ref, down_ref,
    embed3_ref, qkv_high_ref, qkv_low_ref, out2_ref, up2_ref, down2_ref,
):
    embed = jnp.concatenate([embed_ref[...], jnp.zeros((128 - 78, 256), F32)], axis=0)
    high, low = split(jnp.transpose(embed)[:, :ROWS])
    embed3_ref[...] = jnp.concatenate([high, high, low], axis=1)
    for index, ref in enumerate((query_ref, key_ref, value_ref)):
        high, low = split(jnp.transpose(ref[...]))
        qkv_high_ref[index * 256 : (index + 1) * 256, :] = high
        qkv_low_ref[index * 256 : (index + 1) * 256, :] = low
    for source, target in ((out_ref, out2_ref), (up_ref, up2_ref), (down_ref, down2_ref)):
        high, low = split(source[...])
        target[0] = high
        target[1] = low


def layer_norm(values, axis):
    mean = jnp.mean(values, axis=axis, keepdims=True)
    centered = values - mean
    variance = jnp.mean(centered * centered, axis=axis, keepdims=True)
    return centered * lax.rsqrt(variance + EPSILON)


def block_kernel(
    cos_ref, *refs,
):
    pieces = refs[:8]
    embed3_ref, qkv_high_ref, qkv_low_ref, out2_ref, up2_ref, down2_ref = refs[8:14]
    mine_ref, send_ref = refs[14:16]
    edges, fixes, key3, value3, query3 = refs[16:]
    position = lax.axis_index("lon")
    y = position // 8
    z = position % 8
    inverse = 1.0 / cos_ref[0]
    step = 0.5 * STEP_SIZE * inverse * inverse
    for k in range(8):
        for index in range(2):
            half = y if index == 0 else 1 - y
            edges[half * 8 + jnp.bitwise_xor(z, k)] = pieces[k][index, 78:80, :]
    fixes[...] = jnp.zeros_like(fixes)
    for k in range(8):
        for index in range(2):
            half = y if index == 0 else 1 - y
            sector = half * 8 + jnp.bitwise_xor(z, k)
            here = edges[sector]
            west = edges[(sector + 15) % 16]
            east = edges[(sector + 1) % 16]
            first, last = here[0:1], here[1:2]
            west_last, east_first = west[1:2], east[0:1]
            slot = 2 * (2 * k + index)
            fixes[slot : slot + 1, :] = (
                step * (first[:, 78:79] + west_last[:, 78:79]) * (west_last - first)
            )
            fixes[slot + 1 : slot + 2, :] = (
                step * (last[:, 78:79] + east_first[:, 78:79]) * (east_first - last)
            )
    columns = jnp.transpose(fixes[...])[:ROWS]
    lane = lax.broadcasted_iota(jnp.int32, (ROWS, 128), 1)
    hidden = None
    for k in range(8):
        parts = []
        for index in range(2):
            slot = 2 * (2 * k + index)
            part = pieces[k][index]
            part = part + jnp.where(lane == 0, columns[:, slot : slot + 1], 0.0)
            part = part + jnp.where(lane == 127, columns[:, slot + 1 : slot + 2], 0.0)
            parts.append(part)
        high, low = split(jnp.concatenate(parts, axis=1))
        tokens = slice(256 * k, 256 * (k + 1))
        piece_hidden = dot(embed3_ref[...], jnp.concatenate([high, low, high], axis=0))
        normed = split(layer_norm(piece_hidden, 0))
        if k == 0:
            hidden = jnp.transpose(piece_hidden)
            weight = (qkv_high_ref[0:256], qkv_low_ref[0:256])
            scaled = dot3(weight, normed) * (math.log2(math.e) / math.sqrt(256 // HEADS))
            high, low = split(scaled)
            for h in range(HEADS):
                rows = slice(32 * h, 32 * h + 32)
                query3[h, 0:32] = high[rows]
                query3[h, 32:64] = high[rows]
                query3[h, 64:96] = low[rows]
        weight = (qkv_high_ref[256:768], qkv_low_ref[256:768])
        high, low = split(dot3(weight, normed))
        ones = jnp.ones((16, 256), BF16)
        for h in range(HEADS):
            rows = slice(32 * h, 32 * h + 32)
            key3[h, 0:32, tokens] = high[rows]
            key3[h, 32:64, tokens] = low[rows]
            key3[h, 64:96, tokens] = high[rows]
            rows = slice(256 + 32 * h, 256 + 32 * h + 32)
            value3[h, 0:32, tokens] = high[rows]
            value3[h, 32:64, tokens] = low[rows]
            value3[h, 64:80, tokens] = ones
    attended = []
    for h in range(HEADS):
        scores = lax.dot_general(
            query3[h], key3[h], (((0,), (0,)), ((), ())), preferred_element_type=F32
        )
        weights = jnp.exp2(scores - jnp.max(scores, axis=1, keepdims=True))
        high, low = split(weights)
        nt = (((1,), (1,)), ((), ()))
        sums = lax.dot_general(high, value3[h], nt, preferred_element_type=F32)
        sums = sums + lax.dot_general(low, value3[h], nt, preferred_element_type=F32)
        attended.append((sums[:, 0:32] + sums[:, 32:64]) / sums[:, 64:65])
    attended = split(jnp.concatenate(attended, axis=1))
    mixed = hidden + dot3(attended, (out2_ref[0], out2_ref[1]))
    normed = split(layer_norm(mixed, 1))
    activated = split(jax.nn.gelu(dot3(normed, (up2_ref[0], up2_ref[1]))))
    block = mixed + dot3(activated, (down2_ref[0], down2_ref[1]))
    mine_ref[...] = block[:128]
    send_ref[...] = block[128:]


def shape(*dims, dtype=F32):
    return jax.ShapeDtypeStruct(dims, dtype)


def call(kernel, outs, operands, scalars, scratch=(), limit=None, flops=0, moved=0):
    return pl.pallas_call(
        kernel,
        out_shape=outs,
        in_specs=[SMEM] * scalars + [VMEM] * (len(operands) - scalars),
        out_specs=jax.tree.map(lambda _: VMEM, outs),
        scratch_shapes=scratch,
        compiler_params=pltpu.CompilerParams(vmem_limit_bytes=limit),
        cost_estimate=pl.CostEstimate(flops=flops, bytes_accessed=moved, transcendentals=0),
    )(*operands)


def pairs_over(axis_sizes, move):
    lats, lons = axis_sizes
    found = []
    for lat in range(lats):
        for lon in range(lons):
            target = move(lat, lon)
            if 0 <= target[0] < lats:
                found.append((lat * lons + lon, target[0] * lons + target[1]))
    return found


def swap_lon(values, mask):
    count = lax.axis_size("lon")
    return lax.ppermute(values, "lon", [(r, r ^ mask) for r in range(count)])


def on_device(
    fields, diffusivity, w_embed, query_weight, key_weight, value_weight, out_weight, up_weight, down_weight,
):
    sizes = (lax.axis_size("lat"), lax.axis_size("lon"))
    lat = lax.axis_index("lat")
    y = lax.axis_index("lon") // 8
    row = (2 * lat + y).astype(F32)
    faces = jnp.stack([row + 0.5, (2 * lat + 1).astype(F32), (2 * (lat + y)).astype(F32)])
    half = 0.5 * 2 * sizes[0]
    cosines = jnp.cos((CENTER_LAT + (faces - half) * SPACING) * (math.pi / 180.0))

    plane = shape(ROWS, 128)
    pair = shape(2, ROWS, 128)
    both, mine, other = call(pack_kernel, (pair, plane, plane), (fields, diffusivity), 0, moved=400000)
    outward = pairs_over(sizes, lambda a, b: (a + 1 if b < 8 else a - 1, b))
    crossing = pairs_over(sizes, lambda a, b: (a - 1 if b < 8 else a + 1, b ^ 8))
    outer = lax.ppermute(other, ("lat", "lon"), outward)
    partner_outer = lax.ppermute(mine, ("lat", "lon"), crossing)
    partner = swap_lon(both, 8)
    prepared = call(
        weights_kernel,
        (
            shape(256, 3 * ROWS, dtype=BF16),
            shape(768, 256, dtype=BF16),
            shape(768, 256, dtype=BF16),
            shape(2, 256, 256, dtype=BF16),
            shape(2, 256, 1024, dtype=BF16),
            shape(2, 1024, 256, dtype=BF16),
        ),
        (w_embed, query_weight, key_weight, value_weight, out_weight, up_weight, down_weight),
        0,
        limit=24 * 2**20,
        moved=8000000,
    )
    chunk = call(stencil_kernel, pair, (cosines, both, outer, partner, partner_outer), 1, moved=400000)
    far = swap_lon(chunk, 4)
    near = [swap_lon(chunk, k) for k in (1, 2, 3)]
    far_near = [swap_lon(far, k) for k in (1, 2, 3)]
    pieces = [chunk, *near, far, *far_near]
    tile = shape(128, 256)
    own, send = call(
        block_kernel,
        (tile, tile),
        (cosines, *pieces, *prepared),
        1,
        scratch=[
            pltpu.VMEM((16, 2, 128), F32),
            pltpu.VMEM((128, 128), F32),
            pltpu.VMEM((HEADS, 96, 2048), BF16),
            pltpu.VMEM((HEADS, 80, 2048), BF16),
            pltpu.VMEM((HEADS, 96, 256), BF16),
        ],
        limit=48 * 2**20,
        flops=10**10,
        moved=6000000,
    )
    received = swap_lon(send, 8)
    first = jnp.where(y == 0, own, received)
    second = jnp.where(y == 0, received, own)
    return jnp.stack([first, second])


def solution(mesh):
    placed = (P(None, "lat", "lon"), P("lat", "lon"), P(), P(), P(), P(), P(), P(), P())
    return jax.shard_map(
        on_device, mesh=mesh, in_specs=placed, out_specs=P("lat", "lon", None), check_vma=False
    )
```

```python
import functools
import math

import jax
import jax.numpy as jnp
from jax import lax
from jax.experimental import pallas as pl
from jax.experimental.pallas import tpu as pltpu
from jax.sharding import PartitionSpec as P

HEADS = 8
STEP_SIZE = 0.15
CENTER_LAT = 45.0
SPACING = 0.25
EPSILON = 1e-05
ROWS = 80
F32 = jnp.float32
BF16 = jnp.bfloat16
VMEM = pl.BlockSpec(memory_space=pltpu.VMEM)
SMEM = pl.BlockSpec(memory_space=pltpu.SMEM)


def split(values):
    high = values.astype(BF16)
    return high, (values - high.astype(F32)).astype(BF16)


def dot(left, right):
    return jnp.dot(left, right, preferred_element_type=F32)


def dot3(left, right):
    return dot(left[0], right[0]) + dot(left[1], right[0]) + dot(left[0], right[1])


def pack_kernel(fields_ref, kappa_ref, both_ref, mine_ref, other_ref):
    y = lax.axis_index("lon") // 8
    channels = fields_ref.shape[0]
    zero = jnp.zeros((1, 128), F32)
    rows = []
    for row in range(2):
        rows.append(
            jnp.concatenate([fields_ref[:, row, :], kappa_ref[row : row + 1, :], zero], axis=0)
        )
    flag = (jnp.zeros((ROWS, 128), jnp.int32) + y) == 0
    mine = jnp.where(flag, rows[0], rows[1])
    other = jnp.where(flag, rows[1], rows[0])
    both_ref[0] = mine
    both_ref[1] = other
    mine_ref[...] = mine
    other_ref[...] = other


def stencil_kernel(
    cos_ref, both_ref, outer_ref, partner_ref, partner_outer_ref, order_ref, chunk_ref, edges_ref
):
    inverse = 1.0 / cos_ref[0]
    face_inner = cos_ref[1]
    face_outer = cos_ref[2]
    lane = lax.broadcasted_iota(jnp.int32, (ROWS, 128), 1)
    sectors = (
        (both_ref[0], both_ref[1], outer_ref[...]),
        (partner_ref[1], partner_ref[0], partner_outer_ref[...]),
    )
    for index, (q, inner, outer) in enumerate(sectors):
        kappa = q[78:79]
        lat_term = (0.5 * (kappa + inner[78:79]) * face_inner) * (inner - q)
        lat_term = lat_term + (0.5 * (kappa + outer[78:79]) * face_outer) * (outer - q)
        east = pltpu.roll(q, 127, 1)
        flux = (0.5 * (kappa + east[78:79])) * (east - q)
        flux = jnp.where(lane == 127, 0.0, flux)
        lon_term = flux - pltpu.roll(flux, 1, 1)
        updated = q + STEP_SIZE * ((lat_term + lon_term * inverse) * inverse)
        padded = jnp.concatenate([q, jnp.zeros((128 - ROWS, 128), F32)], axis=0)
        turned = jnp.transpose(padded)
        chunk_ref[index] = updated
        chunk_ref[index, 78:79, :] = turned[0:1]
        chunk_ref[index, 79:80, :] = turned[127:128]
        edges_ref[index, 0:1, :] = turned[0:1]
        edges_ref[index, 1:2, :] = turned[127:128]


def first_weights_kernel(*refs):
    sources = refs[:4]
    embed3_ref, qkv_high_ref, qkv_low_ref = refs[5:8]
    embed = jnp.concatenate([sources[0][...], jnp.zeros((128 - 78, 256), F32)], axis=0)
    high, low = split(jnp.transpose(embed)[:, :ROWS])
    embed3_ref[...] = jnp.concatenate([high, high, low], axis=1)
    for index in range(3):
        high, low = split(jnp.transpose(sources[1 + index][...]))
        qkv_high_ref[index * 256 : (index + 1) * 256, :] = high
        qkv_low_ref[index * 256 : (index + 1) * 256, :] = low


def last_weights_kernel(*refs):
    for source, target in zip(refs[:3], refs[4:7]):
        high, low = split(source[...])
        target[0] = high
        target[1] = low
    refs[7][...] = jnp.zeros_like(refs[7])


def layer_norm(values, axis):
    mean = jnp.mean(values, axis=axis, keepdims=True)
    centered = values - mean
    variance = jnp.mean(centered * centered, axis=axis, keepdims=True)
    return centered * lax.rsqrt(variance + EPSILON)


def embed_tokens(columns, embed3_ref):
    high, low = split(columns)
    hidden = dot(embed3_ref[...], jnp.concatenate([high, low, high], axis=0))
    return hidden, split(layer_norm(hidden, 0))


def store_keys(normed, masked, start, qkv_high_ref, qkv_low_ref, key3, value3):
    count = masked.shape[1]
    tokens = slice(start, start + count)
    high, low = split(dot3((qkv_high_ref[256:768], qkv_low_ref[256:768]), normed))
    row = lax.broadcasted_iota(jnp.int32, (16, count), 0)
    mask = jnp.where(jnp.logical_and(masked, row == 0), -1e30, 0.0).astype(BF16)
    ones = jnp.ones((16, count), BF16)
    for h in range(HEADS):
        rows = slice(32 * h, 32 * h + 32)
        key3[h, 0:32, tokens] = high[rows]
        key3[h, 32:64, tokens] = low[rows]
        key3[h, 64:96, tokens] = high[rows]
        key3[h, 96:112, tokens] = mask
        rows = slice(256 + 32 * h, 256 + 32 * h + 32)
        value3[h, 0:32, tokens] = high[rows]
        value3[h, 32:64, tokens] = low[rows]
        value3[h, 64:80, tokens] = ones


def face_fix(step, here, beyond):
    return step * (here[:, 78:79] + beyond[:, 78:79]) * (beyond - here)


def attend(queries, key3, value3, starts):
    nt = (((1,), (1,)), ((), ()))
    found = []
    scores = dot(queries(0), key3[0])
    for h in range(HEADS):
        later = dot(queries(h + 1), key3[h + 1]) if h + 1 < HEADS else None
        largest = jnp.max(scores, axis=1, keepdims=True)
        if starts is not None:
            largest = jnp.maximum(largest, starts(h))
        high, low = split(jnp.exp2(scores - largest))
        sums = lax.dot_general(high, value3[h], nt, preferred_element_type=F32)
        sums = sums + lax.dot_general(low, value3[h], nt, preferred_element_type=F32)
        found.append((largest, sums))
        scores = later
    return found


def place_edges(total, part, slot):
    lane = lax.broadcasted_iota(jnp.int32, (ROWS, 128), 1)
    total = jnp.where(lane == 2 * slot, pltpu.roll(part, 2 * slot, 1), total)
    return jnp.where(lane == 2 * slot + 1, pltpu.roll(part, 2 * slot + 2, 1), total)


def early_kernel(cos_ref, *refs):
    pieces = refs[:5]
    across_ref, embed3_ref, qkv_high_ref, qkv_low_ref = refs[5:9]
    hidden_ref, query3_ref, state_ref, columns_ref, edges_ref = refs[10:15]
    key3, value3 = refs[15:]
    z = lax.axis_index("lon") % 8
    inverse = 1.0 / cos_ref[0]
    step = 0.5 * STEP_SIZE * inverse * inverse
    total = jnp.zeros((ROWS, 128), F32)
    for k in range(5):
        for index in range(2):
            edges_ref[2 * k + index] = pieces[k][index, 78:80, :]
            total = place_edges(total, pieces[k][index], 2 * k + index)
    columns_ref[...] = total
    even = z % 2 == 0
    wraps = jnp.logical_or(z == 0, z == 7).astype(jnp.int32)
    lane = lax.broadcasted_iota(jnp.int32, (ROWS, 128), 1)
    flag = (jnp.zeros((2, 128), jnp.int32) + z % 2) == 0
    fixes = []
    for index in range(2):
        here = pieces[0][index, 78:80, :]
        beside = pieces[1][index, 78:80, :]
        across = across_ref[jnp.where(wraps == 1, 1 - index, index)]
        west = jnp.where(flag, across, beside)
        east = jnp.where(flag, beside, across)
        fixes.append(face_fix(step, here[0:1], west[1:2]))
        fixes.append(face_fix(step, here[1:2], east[0:1]))
    fixes = jnp.transpose(jnp.concatenate(fixes + [jnp.zeros((124, 128), F32)], axis=0))[:ROWS]
    parts = []
    for index in range(2):
        part = pieces[0][index]
        part = part + jnp.where(lane == 0, fixes[:, 2 * index : 2 * index + 1], 0.0)
        part = part + jnp.where(lane == 127, fixes[:, 2 * index + 1 : 2 * index + 2], 0.0)
        parts.append(part)
    for k in range(1, 5):
        parts += [pieces[k][0], pieces[k][1]]
    hidden, normed = embed_tokens(jnp.concatenate(parts, axis=1), embed3_ref)
    hidden_ref[...] = jnp.transpose(hidden[:, :256])
    own = (normed[0][:, :256], normed[1][:, :256])
    scaled = dot3((qkv_high_ref[0:256], qkv_low_ref[0:256]), own)
    scaled = jnp.transpose(scaled * (math.log2(math.e) / math.sqrt(256 // HEADS)))
    high, low = split(scaled)
    row = lax.broadcasted_iota(jnp.int32, (256, 16), 1)
    mask = jnp.where(row == 0, 1.0, 0.0).astype(BF16)
    for h in range(HEADS):
        part = slice(32 * h, 32 * h + 32)
        query3_ref[h] = jnp.concatenate([high[:, part], high[:, part], low[:, part], mask], axis=1)
    lane = lax.broadcasted_iota(jnp.int32, (16, 1280), 1)
    edge = jnp.logical_or(lane % 128 == 0, lane % 128 == 127)
    store_keys(
        normed, jnp.logical_and(edge, lane >= 256), 0, qkv_high_ref, qkv_low_ref, key3, value3
    )
    found = attend(lambda h: query3_ref[h], key3, value3, None)
    for h, (largest, sums) in enumerate(found):
        state_ref[h] = jnp.concatenate([sums, jnp.broadcast_to(largest, (256, 48))], axis=1)


def finish(rows, key3, value3, out2_ref, up2_ref, down2_ref, hidden_ref, query3_ref, state_ref):
    found = attend(
        lambda h: query3_ref[h, rows, :], key3, value3, lambda h: state_ref[h, rows, 80:81]
    )
    attended = []
    for h, (largest, sums) in enumerate(found):
        before = state_ref[h, rows, :]
        sums = sums + before[:, 0:80] * jnp.exp2(before[:, 80:81] - largest)
        attended.append((sums[:, 0:32] + sums[:, 32:64]) / sums[:, 64:65])
    attended = split(jnp.concatenate(attended, axis=1))
    mixed = hidden_ref[rows, :] + dot3(attended, (out2_ref[0], out2_ref[1]))
    normed = split(layer_norm(mixed, 1))
    activated = split(jax.nn.gelu(dot3(normed, (up2_ref[0], up2_ref[1]))))
    return mixed + dot3(activated, (down2_ref[0], down2_ref[1]))


def own_kernel(*refs):
    refs[8][...] = finish(slice(0, 128), *refs[:8])


def late_kernel(cos_ref, *refs):
    pieces = refs[:3]
    embed3_ref, qkv_high_ref, qkv_low_ref, out2_ref, up2_ref, down2_ref = refs[3:9]
    hidden_ref, query3_ref, state_ref, columns_ref, edges_ref = refs[9:14]
    send_ref, key3, value3 = refs[14:17]
    edges, fixes = refs[17:]
    position = lax.axis_index("lon")
    y = position // 8
    z = position % 8
    inverse = 1.0 / cos_ref[0]
    step = 0.5 * STEP_SIZE * inverse * inverse
    total = columns_ref[...]
    for k in range(8):
        for index in range(2):
            half = y if index == 0 else 1 - y
            if k < 5:
                here = edges_ref[2 * k + index]
            else:
                here = pieces[k - 5][index, 78:80, :]
                total = place_edges(total, pieces[k - 5][index], 2 * k + index)
            edges[half * 8 + jnp.bitwise_xor(z, k)] = here
    fixes[...] = jnp.zeros_like(fixes)
    for k in range(8):
        for index in range(2):
            half = y if index == 0 else 1 - y
            sector = half * 8 + jnp.bitwise_xor(z, k)
            here = edges[sector]
            west = edges[(sector + 15) % 16]
            east = edges[(sector + 1) % 16]
            slot = 2 * (2 * k + index)
            fixes[slot : slot + 1, :] = face_fix(step, here[0:1], west[1:2])
            fixes[slot + 1 : slot + 2, :] = face_fix(step, here[1:2], east[0:1])
    total = total + jnp.transpose(fixes[...])[:ROWS]
    parts = [pieces[k][index] for k in range(3) for index in range(2)] + [total]
    hidden, normed = embed_tokens(jnp.concatenate(parts, axis=1), embed3_ref)
    lane = lax.broadcasted_iota(jnp.int32, (16, 896), 1)
    edge = jnp.logical_or(lane % 128 == 0, lane % 128 == 127)
    unused = jnp.logical_or(lane < 768 + 4, lane >= 768 + 32)
    masked = jnp.where(lane < 768, edge.astype(jnp.int32), unused.astype(jnp.int32)) == 1
    store_keys(normed, masked, 0, qkv_high_ref, qkv_low_ref, key3, value3)
    send_ref[...] = finish(
        slice(128, 256), key3, value3, out2_ref, up2_ref, down2_ref, hidden_ref, query3_ref, state_ref
    )


def shape(*dims, dtype=F32):
    return jax.ShapeDtypeStruct(dims, dtype)


def call(kernel, outs, operands, spaces, scratch=(), limit=None, flops=0, moved=0):
    kinds = {"s": SMEM, "v": VMEM, "h": pl.BlockSpec(memory_space=pltpu.HBM)}
    return pl.pallas_call(
        kernel,
        out_shape=outs,
        in_specs=[kinds[letter] for letter in spaces],
        out_specs=jax.tree.map(lambda _: VMEM, outs),
        scratch_shapes=scratch,
        compiler_params=pltpu.CompilerParams(vmem_limit_bytes=limit),
        cost_estimate=pl.CostEstimate(flops=flops, bytes_accessed=moved, transcendentals=0),
    )(*operands)


def pairs_over(axis_sizes, move):
    lats, lons = axis_sizes
    found = []
    for lat in range(lats):
        for lon in range(lons):
            target = move(lat, lon)
            if 0 <= target[0] < lats:
                found.append((lat * lons + lon, target[0] * lons + target[1]))
    return found


def swap_lon(values, mask):
    count = lax.axis_size("lon")
    return lax.ppermute(values, "lon", [(r, r ^ mask) for r in range(count)])


def on_device(
    fields, diffusivity, w_embed, query_weight, key_weight, value_weight, out_weight, up_weight, down_weight,
):
    sizes = (lax.axis_size("lat"), lax.axis_size("lon"))
    lat = lax.axis_index("lat")
    y = lax.axis_index("lon") // 8
    row = (2 * lat + y).astype(F32)
    faces = jnp.stack([row + 0.5, (2 * lat + 1).astype(F32), (2 * (lat + y)).astype(F32)])
    half = 0.5 * 2 * sizes[0]
    cosines = jnp.cos((CENTER_LAT + (faces - half) * SPACING) * (math.pi / 180.0))

    plane = shape(ROWS, 128)
    pair = shape(2, ROWS, 128)
    both, mine, other = call(
        pack_kernel, (pair, plane, plane), (fields, diffusivity), "vv", limit=4 * 2**20, moved=400000
    )
    outward = pairs_over(sizes, lambda a, b: (a + 1 if b < 8 else a - 1, b))
    crossing = pairs_over(sizes, lambda a, b: (a - 1 if b < 8 else a + 1, b ^ 8))
    outer = lax.ppermute(other, ("lat", "lon"), outward)
    partner_outer = lax.ppermute(mine, ("lat", "lon"), crossing)
    partner = swap_lon(both, 8)
    first = call(
        first_weights_kernel,
        (shape(256, 3 * ROWS, dtype=BF16), shape(768, 256, dtype=BF16), shape(768, 256, dtype=BF16)),
        (w_embed, query_weight, key_weight, value_weight, both),
        "vvvvh",
        limit=8 * 2**20,
        moved=2000000,
    )
    chunk, edges = call(
        stencil_kernel,
        (pair, shape(2, 2, 128)),
        (cosines, both, outer, partner, partner_outer, first[0]),
        "svvvvh",
        limit=4 * 2**20,
        moved=400000,
    )
    turn = [(r, (r & 8) | ((r % 8 + (1 if r % 2 else 7)) % 8)) for r in range(sizes[1])]
    across = lax.ppermute(edges, "lon", turn)
    far = swap_lon(chunk, 4)
    near = [swap_lon(chunk, k) for k in (1, 2, 3)]
    far_near = [swap_lon(far, k) for k in (1, 2, 3)]
    *last, order = call(
        last_weights_kernel,
        (
            shape(2, 256, 256, dtype=BF16),
            shape(2, 256, 1024, dtype=BF16),
            shape(2, 1024, 256, dtype=BF16),
            shape(8, 128),
        ),
        (out_weight, up_weight, down_weight, edges),
        "vvvh",
        limit=12 * 2**20,
        moved=5000000,
    )
    early = call(
        early_kernel,
        (
            shape(256, 256),
            shape(HEADS, 256, 112, dtype=BF16),
            shape(HEADS, 256, 128),
            plane,
            shape(16, 2, 128),
        ),
        (cosines, chunk, *near, far, across, *first, order),
        "s" + 9 * "v" + "h",
        scratch=[pltpu.VMEM((HEADS, 112, 1280), BF16), pltpu.VMEM((HEADS, 80, 1280), BF16)],
        limit=40 * 2**20,
        flops=5 * 10**9,
        moved=3000000,
    )
    tile = shape(128, 256)
    send, *keys = call(
        late_kernel,
        (tile, shape(HEADS, 112, 896, dtype=BF16), shape(HEADS, 80, 896, dtype=BF16)),
        (cosines, *far_near, *first, *last, *early),
        "s" + 14 * "v",
        scratch=[pltpu.VMEM((16, 2, 128), F32), pltpu.VMEM((128, 128), F32)],
        limit=36 * 2**20,
        flops=5 * 10**9,
        moved=6000000,
    )
    own = call(
        own_kernel,
        tile,
        (*keys, *last, *early[:3]),
        8 * "v",
        limit=36 * 2**20,
        flops=3 * 10**9,
        moved=6000000,
    )
    received = swap_lon(send, 8)
    first = jnp.where(y == 0, own, received)
    second = jnp.where(y == 0, received, own)
    return jnp.stack([first, second])


def solution(mesh):
    placed = (P(None, "lat", "lon"), P("lat", "lon"), P(), P(), P(), P(), P(), P(), P())
    return jax.shard_map(
        on_device, mesh=mesh, in_specs=placed, out_specs=P("lat", "lon", None), check_vma=False
    )
```

```python
import functools
import math

import jax
import jax.numpy as jnp
from jax import lax
from jax.experimental import pallas as pl
from jax.experimental.pallas import tpu as pltpu
from jax.sharding import PartitionSpec as P

HEADS = 8
STEP_SIZE = 0.15
CENTER_LAT = 45.0
SPACING = 0.25
EPSILON = 1e-05
PARTNERS = (0, 1, 2, 3, 7, 6, 5, 4)
ROWS = 80
F32 = jnp.float32
BF16 = jnp.bfloat16
VMEM = pl.BlockSpec(memory_space=pltpu.VMEM)
SMEM = pl.BlockSpec(memory_space=pltpu.SMEM)


def split(values):
    high = values.astype(BF16)
    return high, (values - high.astype(F32)).astype(BF16)


def dot(left, right):
    return jnp.dot(left, right, preferred_element_type=F32)


def dot3(left, right):
    return dot(left[0], right[0]) + dot(left[1], right[0]) + dot(left[0], right[1])


def pack_kernel(fields_ref, kappa_ref, both_ref):
    y = lax.axis_index("lon") // 8
    channels = fields_ref.shape[0]
    zero = jnp.zeros((1, 128), F32)
    rows = []
    for row in range(2):
        rows.append(
            jnp.concatenate([fields_ref[:, row, :], kappa_ref[row : row + 1, :], zero], axis=0)
        )
    flag = (jnp.zeros((ROWS, 128), jnp.int32) + y) == 0
    mine = jnp.where(flag, rows[0], rows[1])
    other = jnp.where(flag, rows[1], rows[0])
    both_ref[0] = mine
    both_ref[1] = other


def stencil_kernel(
    cos_ref, both_ref, outer_ref, partner_ref, partner_outer_ref, order_ref, chunk_ref
):
    inverse = 1.0 / cos_ref[0]
    face_inner = cos_ref[1]
    face_outer = cos_ref[2]
    lane = lax.broadcasted_iota(jnp.int32, (ROWS, 128), 1)
    sectors = (
        (both_ref[0], both_ref[1], outer_ref[...]),
        (partner_ref[1], partner_ref[0], partner_outer_ref[...]),
    )
    for index, (q, inner, outer) in enumerate(sectors):
        kappa = q[78:79]
        lat_term = (0.5 * (kappa + inner[78:79]) * face_inner) * (inner - q)
        lat_term = lat_term + (0.5 * (kappa + outer[78:79]) * face_outer) * (outer - q)
        east = pltpu.roll(q, 127, 1)
        flux = (0.5 * (kappa + east[78:79])) * (east - q)
        flux = jnp.where(lane == 127, 0.0, flux)
        lon_term = flux - pltpu.roll(flux, 1, 1)
        updated = q + STEP_SIZE * ((lat_term + lon_term * inverse) * inverse)
        padded = jnp.concatenate([q, jnp.zeros((128 - ROWS, 128), F32)], axis=0)
        turned = jnp.transpose(padded)
        chunk_ref[index] = updated
        chunk_ref[index, 78:79, :] = turned[0:1]
        chunk_ref[index, 79:80, :] = turned[127:128]


def first_weights_kernel(*refs):
    sources = refs[:4]
    embed3_ref, qkv_high_ref, qkv_low_ref = refs[5:8]
    embed = jnp.concatenate([sources[0][...], jnp.zeros((128 - 78, 256), F32)], axis=0)
    high, low = split(jnp.transpose(embed)[:, :ROWS])
    embed3_ref[...] = jnp.concatenate([high, high, low], axis=1)
    for index in range(3):
        high, low = split(jnp.transpose(sources[1 + index][...]))
        qkv_high_ref[index * 256 : (index + 1) * 256, :] = high
        qkv_low_ref[index * 256 : (index + 1) * 256, :] = low


def last_weights_kernel(*refs):
    for source, target in zip(refs[:3], refs[4:7]):
        high, low = split(source[...])
        target[0] = high
        target[1] = low
    refs[7][...] = jnp.zeros_like(refs[7])


def layer_norm(values, axis):
    mean = jnp.mean(values, axis=axis, keepdims=True)
    centered = values - mean
    variance = jnp.mean(centered * centered, axis=axis, keepdims=True)
    return centered * lax.rsqrt(variance + EPSILON)


def embed_tokens(columns, embed3_ref):
    high, low = split(columns)
    hidden = dot(embed3_ref[...], jnp.concatenate([high, low, high], axis=0))
    return hidden, split(layer_norm(hidden, 0))


def store_keys(normed, masked, start, qkv_high_ref, qkv_low_ref, key3, value3):
    count = masked.shape[1]
    tokens = slice(start, start + count)
    high, low = split(dot3((qkv_high_ref[256:768], qkv_low_ref[256:768]), normed))
    row = lax.broadcasted_iota(jnp.int32, (16, count), 0)
    mask = jnp.where(jnp.logical_and(masked, row == 0), -1e30, 0.0).astype(BF16)
    ones = jnp.ones((16, count), BF16)
    for h in range(HEADS):
        rows = slice(32 * h, 32 * h + 32)
        key3[h, 0:32, tokens] = high[rows]
        key3[h, 32:64, tokens] = low[rows]
        key3[h, 64:96, tokens] = high[rows]
        key3[h, 96:112, tokens] = mask
        rows = slice(256 + 32 * h, 256 + 32 * h + 32)
        value3[h, 0:32, tokens] = high[rows]
        value3[h, 32:64, tokens] = low[rows]
        value3[h, 64:80, tokens] = ones


def face_fix(step, here, beyond):
    return step * (here[:, 78:79] + beyond[:, 78:79]) * (beyond - here)


def attend(queries, key3, value3, starts):
    nt = (((1,), (1,)), ((), ()))
    found = []
    scores = dot(queries(0), key3[0])
    for h in range(HEADS):
        later = dot(queries(h + 1), key3[h + 1]) if h + 1 < HEADS else None
        largest = jnp.max(scores, axis=1, keepdims=True)
        if starts is not None:
            largest = jnp.maximum(largest, starts(h))
        high, low = split(jnp.exp2(scores - largest))
        sums = lax.dot_general(high, value3[h], nt, preferred_element_type=F32)
        sums = sums + lax.dot_general(low, value3[h], nt, preferred_element_type=F32)
        found.append((largest, sums))
        scores = later
    return found


def place_edges(total, part, slot):
    lane = lax.broadcasted_iota(jnp.int32, (ROWS, 128), 1)
    total = jnp.where(lane == 2 * slot, pltpu.roll(part, 2 * slot, 1), total)
    return jnp.where(lane == 2 * slot + 1, pltpu.roll(part, 2 * slot + 2, 1), total)


def early_kernel(cos_ref, *refs):
    pieces = refs[:5]
    embed3_ref, qkv_high_ref, qkv_low_ref = refs[5:8]
    hidden_ref, query3_ref, state_ref, columns_ref, edges_ref = refs[9:14]
    key3, value3 = refs[14:]
    z = lax.axis_index("lon") % 8
    inverse = 1.0 / cos_ref[0]
    step = 0.5 * STEP_SIZE * inverse * inverse
    total = jnp.zeros((ROWS, 128), F32)
    for k in range(5):
        for index in range(2):
            edges_ref[2 * k + index] = pieces[k][index, 78:80, :]
            total = place_edges(total, pieces[k][index], 2 * k + index)
    columns_ref[...] = total
    wraps = jnp.logical_or(z == 0, z == 7).astype(jnp.int32)
    lane = lax.broadcasted_iota(jnp.int32, (ROWS, 128), 1)
    flag = (jnp.zeros((2, 128), jnp.int32) + z % 2) == 0
    outer = (jnp.zeros((2, 128), jnp.int32) + ((z + 1) // 2) % 2) == 0
    fixes = []
    for index in range(2):
        here = pieces[0][index, 78:80, :]
        beside = pieces[1][index, 78:80, :]
        wrapped = jnp.where(wraps == 1, 1 - index, index)
        across = jnp.where(outer, pieces[4][wrapped, 78:80, :], pieces[3][index, 78:80, :])
        west = jnp.where(flag, across, beside)
        east = jnp.where(flag, beside, across)
        fixes.append(face_fix(step, here[0:1], west[1:2]))
        fixes.append(face_fix(step, here[1:2], east[0:1]))
    fixes = jnp.transpose(jnp.concatenate(fixes + [jnp.zeros((124, 128), F32)], axis=0))[:ROWS]
    parts = []
    for index in range(2):
        part = pieces[0][index]
        part = part + jnp.where(lane == 0, fixes[:, 2 * index : 2 * index + 1], 0.0)
        part = part + jnp.where(lane == 127, fixes[:, 2 * index + 1 : 2 * index + 2], 0.0)
        parts.append(part)
    for k in range(1, 5):
        parts += [pieces[k][0], pieces[k][1]]
    hidden, normed = embed_tokens(jnp.concatenate(parts, axis=1), embed3_ref)
    hidden_ref[...] = jnp.transpose(hidden[:, :256])
    own = (normed[0][:, :256], normed[1][:, :256])
    scaled = dot3((qkv_high_ref[0:256], qkv_low_ref[0:256]), own)
    scaled = jnp.transpose(scaled * (math.log2(math.e) / math.sqrt(256 // HEADS)))
    high, low = split(scaled)
    row = lax.broadcasted_iota(jnp.int32, (256, 16), 1)
    mask = jnp.where(row == 0, 1.0, 0.0).astype(BF16)
    for h in range(HEADS):
        part = slice(32 * h, 32 * h + 32)
        query3_ref[h] = jnp.concatenate([high[:, part], high[:, part], low[:, part], mask], axis=1)
    lane = lax.broadcasted_iota(jnp.int32, (16, 1280), 1)
    edge = jnp.logical_or(lane % 128 == 0, lane % 128 == 127)
    store_keys(
        normed, jnp.logical_and(edge, lane >= 256), 0, qkv_high_ref, qkv_low_ref, key3, value3
    )
    found = attend(lambda h: query3_ref[h], key3, value3, None)
    for h, (largest, sums) in enumerate(found):
        state_ref[h] = jnp.concatenate([sums, jnp.broadcast_to(largest, (256, 48))], axis=1)


def finish(rows, key3, value3, out2_ref, up2_ref, down2_ref, hidden_ref, query3_ref, state_ref):
    found = attend(
        lambda h: query3_ref[h, rows, :], key3, value3, lambda h: state_ref[h, rows, 80:81]
    )
    attended = []
    for h, (largest, sums) in enumerate(found):
        before = state_ref[h, rows, :]
        sums = sums + before[:, 0:80] * jnp.exp2(before[:, 80:81] - largest)
        attended.append((sums[:, 0:32] + sums[:, 32:64]) / sums[:, 64:65])
    attended = split(jnp.concatenate(attended, axis=1))
    mixed = hidden_ref[rows, :] + dot3(attended, (out2_ref[0], out2_ref[1]))
    normed = split(layer_norm(mixed, 1))
    activated = split(jax.nn.gelu(dot3(normed, (up2_ref[0], up2_ref[1]))))
    return mixed + dot3(activated, (down2_ref[0], down2_ref[1]))


def own_kernel(*refs):
    refs[8][...] = finish(slice(0, 128), *refs[:8])


def late_kernel(cos_ref, *refs):
    pieces = refs[:3]
    embed3_ref, qkv_high_ref, qkv_low_ref, out2_ref, up2_ref, down2_ref = refs[3:9]
    hidden_ref, query3_ref, state_ref, columns_ref, edges_ref = refs[9:14]
    send_ref, key3, value3 = refs[14:17]
    edges, fixes = refs[17:]
    position = lax.axis_index("lon")
    y = position // 8
    z = position % 8
    inverse = 1.0 / cos_ref[0]
    step = 0.5 * STEP_SIZE * inverse * inverse
    total = columns_ref[...]
    for k in range(8):
        for index in range(2):
            half = y if index == 0 else 1 - y
            if k < 5:
                here = edges_ref[2 * k + index]
            else:
                here = pieces[k - 5][index, 78:80, :]
                total = place_edges(total, pieces[k - 5][index], 2 * k + index)
            edges[half * 8 + jnp.bitwise_xor(z, PARTNERS[k])] = here
    fixes[...] = jnp.zeros_like(fixes)
    for k in range(8):
        for index in range(2):
            half = y if index == 0 else 1 - y
            sector = half * 8 + jnp.bitwise_xor(z, PARTNERS[k])
            here = edges[sector]
            west = edges[(sector + 15) % 16]
            east = edges[(sector + 1) % 16]
            slot = 2 * (2 * k + index)
            fixes[slot : slot + 1, :] = face_fix(step, here[0:1], west[1:2])
            fixes[slot + 1 : slot + 2, :] = face_fix(step, here[1:2], east[0:1])
    total = total + jnp.transpose(fixes[...])[:ROWS]
    parts = [pieces[k][index] for k in range(3) for index in range(2)] + [total]
    hidden, normed = embed_tokens(jnp.concatenate(parts, axis=1), embed3_ref)
    lane = lax.broadcasted_iota(jnp.int32, (16, 896), 1)
    edge = jnp.logical_or(lane % 128 == 0, lane % 128 == 127)
    unused = jnp.logical_or(lane < 768 + 4, lane >= 768 + 32)
    masked = jnp.where(lane < 768, edge.astype(jnp.int32), unused.astype(jnp.int32)) == 1
    store_keys(normed, masked, 0, qkv_high_ref, qkv_low_ref, key3, value3)
    send_ref[...] = finish(
        slice(128, 256), key3, value3, out2_ref, up2_ref, down2_ref, hidden_ref, query3_ref, state_ref
    )


def shape(*dims, dtype=F32):
    return jax.ShapeDtypeStruct(dims, dtype)


def call(kernel, outs, operands, spaces, scratch=(), limit=None, flops=0, moved=0):
    kinds = {"s": SMEM, "v": VMEM, "h": pl.BlockSpec(memory_space=pltpu.HBM)}
    return pl.pallas_call(
        kernel,
        out_shape=outs,
        in_specs=[kinds[letter] for letter in spaces],
        out_specs=jax.tree.map(lambda _: VMEM, outs),
        scratch_shapes=scratch,
        compiler_params=pltpu.CompilerParams(vmem_limit_bytes=limit),
        cost_estimate=pl.CostEstimate(flops=flops, bytes_accessed=moved, transcendentals=0),
    )(*operands)


def pairs_over(axis_sizes, move):
    lats, lons = axis_sizes
    found = []
    for lat in range(lats):
        for lon in range(lons):
            target = move(lat, lon)
            if 0 <= target[0] < lats:
                found.append((lat * lons + lon, target[0] * lons + target[1]))
    return found


def swap_lon(values, mask):
    count = lax.axis_size("lon")
    return lax.ppermute(values, "lon", [(r, r ^ mask) for r in range(count)])


def on_device(
    fields, diffusivity, w_embed, query_weight, key_weight, value_weight, out_weight, up_weight, down_weight,
):
    sizes = (lax.axis_size("lat"), lax.axis_size("lon"))
    lat = lax.axis_index("lat")
    y = lax.axis_index("lon") // 8
    row = (2 * lat + y).astype(F32)
    faces = jnp.stack([row + 0.5, (2 * lat + 1).astype(F32), (2 * (lat + y)).astype(F32)])
    half = 0.5 * 2 * sizes[0]
    cosines = jnp.cos((CENTER_LAT + (faces - half) * SPACING) * (math.pi / 180.0))

    plane = shape(ROWS, 128)
    pair = shape(2, ROWS, 128)
    both = call(
        pack_kernel, pair, (fields, diffusivity), "vv", limit=4 * 2**20, moved=400000
    )
    outward = pairs_over(sizes, lambda a, b: (a + 1 if b < 8 else a - 1, b))
    crossing = pairs_over(sizes, lambda a, b: (a - 1 if b < 8 else a + 1, b ^ 8))
    partner = swap_lon(both, 8)
    outer = lax.ppermute(both[1], ("lat", "lon"), outward)
    partner_outer = lax.ppermute(both[0], ("lat", "lon"), crossing)
    first = call(
        first_weights_kernel,
        (shape(256, 3 * ROWS, dtype=BF16), shape(768, 256, dtype=BF16), shape(768, 256, dtype=BF16)),
        (w_embed, query_weight, key_weight, value_weight, both),
        "vvvvh",
        limit=8 * 2**20,
        moved=2000000,
    )
    chunk = call(
        stencil_kernel,
        pair,
        (cosines, both, outer, partner, partner_outer, first[0]),
        "svvvvh",
        limit=4 * 2**20,
        moved=400000,
    )
    far = swap_lon(chunk, 7)
    near = [swap_lon(chunk, k) for k in (1, 2, 3)]
    far_near = [swap_lon(far, k) for k in (1, 2, 3)]
    *last, order = call(
        last_weights_kernel,
        (
            shape(2, 256, 256, dtype=BF16),
            shape(2, 256, 1024, dtype=BF16),
            shape(2, 1024, 256, dtype=BF16),
            shape(8, 128),
        ),
        (out_weight, up_weight, down_weight, chunk),
        "vvvh",
        limit=12 * 2**20,
        moved=5000000,
    )
    early = call(
        early_kernel,
        (
            shape(256, 256),
            shape(HEADS, 256, 112, dtype=BF16),
            shape(HEADS, 256, 128),
            plane,
            shape(16, 2, 128),
        ),
        (cosines, chunk, *near, far, *first, order),
        "s" + 8 * "v" + "h",
        scratch=[pltpu.VMEM((HEADS, 112, 1280), BF16), pltpu.VMEM((HEADS, 80, 1280), BF16)],
        limit=40 * 2**20,
        flops=5 * 10**9,
        moved=3000000,
    )
    tile = shape(128, 256)
    send, *keys = call(
        late_kernel,
        (tile, shape(HEADS, 112, 896, dtype=BF16), shape(HEADS, 80, 896, dtype=BF16)),
        (cosines, *far_near, *first, *last, *early),
        "s" + 14 * "v",
        scratch=[pltpu.VMEM((16, 2, 128), F32), pltpu.VMEM((128, 128), F32)],
        limit=36 * 2**20,
        flops=5 * 10**9,
        moved=6000000,
    )
    own = call(
        own_kernel,
        tile,
        (*keys, *last, *early[:3]),
        8 * "v",
        limit=36 * 2**20,
        flops=3 * 10**9,
        moved=6000000,
    )
    received = swap_lon(send, 8)
    first = jnp.where(y == 0, own, received)
    second = jnp.where(y == 0, received, own)
    return jnp.stack([first, second])


def solution(mesh):
    placed = (P(None, "lat", "lon"), P("lat", "lon"), P(), P(), P(), P(), P(), P(), P())
    return jax.shard_map(
        on_device, mesh=mesh, in_specs=placed, out_specs=P("lat", "lon", None), check_vma=False
    )
```

```python
import functools
import math

import jax
import jax.numpy as jnp
from jax import lax
from jax.experimental import pallas as pl
from jax.experimental.pallas import tpu as pltpu
from jax.sharding import PartitionSpec as P

HEADS = 8
STEP_SIZE = 0.15
CENTER_LAT = 45.0
SPACING = 0.25
EPSILON = 1e-05
PARTNERS = (0, 1, 3, 7, 2, 6, 5, 4)
ROWS = 80
F32 = jnp.float32
BF16 = jnp.bfloat16
VMEM = pl.BlockSpec(memory_space=pltpu.VMEM)
SMEM = pl.BlockSpec(memory_space=pltpu.SMEM)


def split(values):
    high = values.astype(BF16)
    return high, (values - high.astype(F32)).astype(BF16)


def dot(left, right):
    return jnp.dot(left, right, preferred_element_type=F32)


def dot3(left, right):
    return dot(left[0], right[0]) + dot(left[1], right[0]) + dot(left[0], right[1])


def pack_kernel(fields_ref, kappa_ref, both_ref):
    y = lax.axis_index("lon") // 8
    channels = fields_ref.shape[0]
    zero = jnp.zeros((1, 128), F32)
    rows = []
    for row in range(2):
        rows.append(
            jnp.concatenate([fields_ref[:, row, :], kappa_ref[row : row + 1, :], zero], axis=0)
        )
    flag = (jnp.zeros((ROWS, 128), jnp.int32) + y) == 0
    mine = jnp.where(flag, rows[0], rows[1])
    other = jnp.where(flag, rows[1], rows[0])
    both_ref[0] = mine
    both_ref[1] = other


def stencil_kernel(
    cos_ref, both_ref, outer_ref, partner_ref, partner_outer_ref, chunk_ref
):
    inverse = 1.0 / cos_ref[0]
    face_inner = cos_ref[1]
    face_outer = cos_ref[2]
    lane = lax.broadcasted_iota(jnp.int32, (ROWS, 128), 1)
    sectors = (
        (both_ref[0], both_ref[1], outer_ref[...]),
        (partner_ref[1], partner_ref[0], partner_outer_ref[...]),
    )
    for index, (q, inner, outer) in enumerate(sectors):
        kappa = q[78:79]
        lat_term = (0.5 * (kappa + inner[78:79]) * face_inner) * (inner - q)
        lat_term = lat_term + (0.5 * (kappa + outer[78:79]) * face_outer) * (outer - q)
        east = pltpu.roll(q, 127, 1)
        flux = (0.5 * (kappa + east[78:79])) * (east - q)
        flux = jnp.where(lane == 127, 0.0, flux)
        lon_term = flux - pltpu.roll(flux, 1, 1)
        updated = q + STEP_SIZE * ((lat_term + lon_term * inverse) * inverse)
        padded = jnp.concatenate([q, jnp.zeros((128 - ROWS, 128), F32)], axis=0)
        turned = jnp.transpose(padded)
        chunk_ref[index] = updated
        chunk_ref[index, 78:79, :] = turned[0:1]
        chunk_ref[index, 79:80, :] = turned[127:128]


def first_weights_kernel(*refs):
    sources = refs[:4]
    embed3_ref, qkv_high_ref, qkv_low_ref = refs[5:8]
    embed = jnp.concatenate([sources[0][...], jnp.zeros((128 - 78, 256), F32)], axis=0)
    high, low = split(jnp.transpose(embed)[:, :ROWS])
    embed3_ref[...] = jnp.concatenate([high, high, low], axis=1)
    for index in range(3):
        high, low = split(jnp.transpose(sources[1 + index][...]))
        qkv_high_ref[index * 256 : (index + 1) * 256, :] = high
        qkv_low_ref[index * 256 : (index + 1) * 256, :] = low


def last_weights_kernel(*refs):
    for source, target in zip(refs[:3], refs[4:7]):
        high, low = split(source[...])
        target[0] = high
        target[1] = low
    refs[7][...] = jnp.zeros_like(refs[7])


def layer_norm(values, axis):
    mean = jnp.mean(values, axis=axis, keepdims=True)
    centered = values - mean
    variance = jnp.mean(centered * centered, axis=axis, keepdims=True)
    return centered * lax.rsqrt(variance + EPSILON)


def embed_tokens(columns, embed3_ref):
    high, low = split(columns)
    hidden = dot(embed3_ref[...], jnp.concatenate([high, low, high], axis=0))
    return hidden, split(layer_norm(hidden, 0))


def store_keys(normed, masked, start, qkv_high_ref, qkv_low_ref, key3, value3):
    count = masked.shape[1]
    tokens = slice(start, start + count)
    high, low = split(dot3((qkv_high_ref[256:768], qkv_low_ref[256:768]), normed))
    row = lax.broadcasted_iota(jnp.int32, (16, count), 0)
    mask = jnp.where(jnp.logical_and(masked, row == 0), -1e30, 0.0).astype(BF16)
    ones = jnp.ones((16, count), BF16)
    for h in range(HEADS):
        rows = slice(32 * h, 32 * h + 32)
        key3[h, 0:32, tokens] = high[rows]
        key3[h, 32:64, tokens] = low[rows]
        key3[h, 64:96, tokens] = high[rows]
        key3[h, 96:112, tokens] = mask
        rows = slice(256 + 32 * h, 256 + 32 * h + 32)
        value3[h, 0:32, tokens] = high[rows]
        value3[h, 32:64, tokens] = low[rows]
        value3[h, 64:80, tokens] = ones


def face_fix(step, here, beyond):
    return step * (here[:, 78:79] + beyond[:, 78:79]) * (beyond - here)


def attend(queries, key3, value3, starts):
    nt = (((1,), (1,)), ((), ()))
    found = []
    scores = dot(queries(0), key3[0])
    for h in range(HEADS):
        later = dot(queries(h + 1), key3[h + 1]) if h + 1 < HEADS else None
        largest = jnp.max(scores, axis=1, keepdims=True)
        if starts is not None:
            largest = jnp.maximum(largest, starts(h))
        high, low = split(jnp.exp2(scores - largest))
        sums = lax.dot_general(high, value3[h], nt, preferred_element_type=F32)
        sums = sums + lax.dot_general(low, value3[h], nt, preferred_element_type=F32)
        found.append((largest, sums))
        scores = later
    return found


def place_edges(total, part, slot):
    lane = lax.broadcasted_iota(jnp.int32, (ROWS, 128), 1)
    total = jnp.where(lane == 2 * slot, pltpu.roll(part, 2 * slot, 1), total)
    return jnp.where(lane == 2 * slot + 1, pltpu.roll(part, 2 * slot + 2, 1), total)


def early_kernel(cos_ref, *refs):
    pieces = refs[:4]
    embed3_ref, qkv_high_ref, qkv_low_ref = refs[4:7]
    hidden_ref, query3_ref, state_ref, columns_ref, edges_ref = refs[8:13]
    key3, value3 = refs[13:]
    z = lax.axis_index("lon") % 8
    inverse = 1.0 / cos_ref[0]
    step = 0.5 * STEP_SIZE * inverse * inverse
    total = jnp.zeros((ROWS, 128), F32)
    for k in range(4):
        for index in range(2):
            edges_ref[2 * k + index] = pieces[k][index, 78:80, :]
            total = place_edges(total, pieces[k][index], 2 * k + index)
    columns_ref[...] = total
    wraps = jnp.logical_or(z == 0, z == 7).astype(jnp.int32)
    lane = lax.broadcasted_iota(jnp.int32, (ROWS, 128), 1)
    flag = (jnp.zeros((2, 128), jnp.int32) + z % 2) == 0
    outer = (jnp.zeros((2, 128), jnp.int32) + ((z + 1) // 2) % 2) == 0
    fixes = []
    for index in range(2):
        here = pieces[0][index, 78:80, :]
        beside = pieces[1][index, 78:80, :]
        wrapped = jnp.where(wraps == 1, 1 - index, index)
        across = jnp.where(outer, pieces[3][wrapped, 78:80, :], pieces[2][index, 78:80, :])
        west = jnp.where(flag, across, beside)
        east = jnp.where(flag, beside, across)
        fixes.append(face_fix(step, here[0:1], west[1:2]))
        fixes.append(face_fix(step, here[1:2], east[0:1]))
    fixes = jnp.transpose(jnp.concatenate(fixes + [jnp.zeros((124, 128), F32)], axis=0))[:ROWS]
    parts = []
    for index in range(2):
        part = pieces[0][index]
        part = part + jnp.where(lane == 0, fixes[:, 2 * index : 2 * index + 1], 0.0)
        part = part + jnp.where(lane == 127, fixes[:, 2 * index + 1 : 2 * index + 2], 0.0)
        parts.append(part)
    for k in range(1, 4):
        parts += [pieces[k][0], pieces[k][1]]
    hidden, normed = embed_tokens(jnp.concatenate(parts, axis=1), embed3_ref)
    hidden_ref[...] = jnp.transpose(hidden[:, :256])
    own = (normed[0][:, :256], normed[1][:, :256])
    scaled = dot3((qkv_high_ref[0:256], qkv_low_ref[0:256]), own)
    scaled = jnp.transpose(scaled * (math.log2(math.e) / math.sqrt(256 // HEADS)))
    high, low = split(scaled)
    row = lax.broadcasted_iota(jnp.int32, (256, 16), 1)
    mask = jnp.where(row == 0, 1.0, 0.0).astype(BF16)
    for h in range(HEADS):
        part = slice(32 * h, 32 * h + 32)
        query3_ref[h] = jnp.concatenate([high[:, part], high[:, part], low[:, part], mask], axis=1)
    lane = lax.broadcasted_iota(jnp.int32, (16, 1024), 1)
    edge = jnp.logical_or(lane % 128 == 0, lane % 128 == 127)
    store_keys(
        normed, jnp.logical_and(edge, lane >= 256), 0, qkv_high_ref, qkv_low_ref, key3, value3
    )
    found = attend(lambda h: query3_ref[h], key3, value3, None)
    for h, (largest, sums) in enumerate(found):
        state_ref[h] = jnp.concatenate([sums, jnp.broadcast_to(largest, (256, 48))], axis=1)


def finish(rows, key3, value3, out2_ref, up2_ref, down2_ref, hidden_ref, query3_ref, state_ref):
    found = attend(
        lambda h: query3_ref[h, rows, :], key3, value3, lambda h: state_ref[h, rows, 80:81]
    )
    attended = []
    for h, (largest, sums) in enumerate(found):
        before = state_ref[h, rows, :]
        sums = sums + before[:, 0:80] * jnp.exp2(before[:, 80:81] - largest)
        attended.append((sums[:, 0:32] + sums[:, 32:64]) / sums[:, 64:65])
    attended = split(jnp.concatenate(attended, axis=1))
    mixed = hidden_ref[rows, :] + dot3(attended, (out2_ref[0], out2_ref[1]))
    normed = split(layer_norm(mixed, 1))
    activated = split(jax.nn.gelu(dot3(normed, (up2_ref[0], up2_ref[1]))))
    return mixed + dot3(activated, (down2_ref[0], down2_ref[1]))


def own_kernel(*refs):
    refs[8][...] = finish(slice(0, 128), *refs[:8])


def late_kernel(cos_ref, *refs):
    pieces = refs[:4]
    embed3_ref, qkv_high_ref, qkv_low_ref, out2_ref, up2_ref, down2_ref = refs[4:10]
    hidden_ref, query3_ref, state_ref, columns_ref, edges_ref = refs[10:15]
    send_ref, key3, value3 = refs[15:18]
    edges, fixes = refs[18:]
    position = lax.axis_index("lon")
    y = position // 8
    z = position % 8
    inverse = 1.0 / cos_ref[0]
    step = 0.5 * STEP_SIZE * inverse * inverse
    total = columns_ref[...]
    for k in range(8):
        for index in range(2):
            half = y if index == 0 else 1 - y
            if k < 4:
                here = edges_ref[2 * k + index]
            else:
                here = pieces[k - 4][index, 78:80, :]
                total = place_edges(total, pieces[k - 4][index], 2 * k + index)
            edges[half * 8 + jnp.bitwise_xor(z, PARTNERS[k])] = here
    fixes[...] = jnp.zeros_like(fixes)
    for k in range(8):
        for index in range(2):
            half = y if index == 0 else 1 - y
            sector = half * 8 + jnp.bitwise_xor(z, PARTNERS[k])
            here = edges[sector]
            west = edges[(sector + 15) % 16]
            east = edges[(sector + 1) % 16]
            slot = 2 * (2 * k + index)
            fixes[slot : slot + 1, :] = face_fix(step, here[0:1], west[1:2])
            fixes[slot + 1 : slot + 2, :] = face_fix(step, here[1:2], east[0:1])
    total = total + jnp.transpose(fixes[...])[:ROWS]
    parts = [pieces[k][index] for k in range(4) for index in range(2)] + [total]
    hidden, normed = embed_tokens(jnp.concatenate(parts, axis=1), embed3_ref)
    lane = lax.broadcasted_iota(jnp.int32, (16, 1152), 1)
    edge = jnp.logical_or(lane % 128 == 0, lane % 128 == 127)
    unused = jnp.logical_or(lane < 1024 + 4, lane >= 1024 + 32)
    masked = jnp.where(lane < 1024, edge.astype(jnp.int32), unused.astype(jnp.int32)) == 1
    store_keys(normed, masked, 0, qkv_high_ref, qkv_low_ref, key3, value3)
    send_ref[...] = finish(
        slice(128, 256), key3, value3, out2_ref, up2_ref, down2_ref, hidden_ref, query3_ref, state_ref
    )


def shape(*dims, dtype=F32):
    return jax.ShapeDtypeStruct(dims, dtype)


def call(kernel, outs, operands, spaces, scratch=(), limit=None, flops=0, moved=0):
    kinds = {"s": SMEM, "v": VMEM, "h": pl.BlockSpec(memory_space=pltpu.HBM)}
    return pl.pallas_call(
        kernel,
        out_shape=outs,
        in_specs=[kinds[letter] for letter in spaces],
        out_specs=jax.tree.map(lambda _: VMEM, outs),
        scratch_shapes=scratch,
        compiler_params=pltpu.CompilerParams(vmem_limit_bytes=limit),
        cost_estimate=pl.CostEstimate(flops=flops, bytes_accessed=moved, transcendentals=0),
    )(*operands)


def pairs_over(axis_sizes, move):
    lats, lons = axis_sizes
    found = []
    for lat in range(lats):
        for lon in range(lons):
            target = move(lat, lon)
            if 0 <= target[0] < lats:
                found.append((lat * lons + lon, target[0] * lons + target[1]))
    return found


def swap_lon(values, mask):
    count = lax.axis_size("lon")
    return lax.ppermute(values, "lon", [(r, r ^ mask) for r in range(count)])


def on_device(
    fields, diffusivity, w_embed, query_weight, key_weight, value_weight, out_weight, up_weight, down_weight,
):
    sizes = (lax.axis_size("lat"), lax.axis_size("lon"))
    lat = lax.axis_index("lat")
    y = lax.axis_index("lon") // 8
    row = (2 * lat + y).astype(F32)
    faces = jnp.stack([row + 0.5, (2 * lat + 1).astype(F32), (2 * (lat + y)).astype(F32)])
    half = 0.5 * 2 * sizes[0]
    cosines = jnp.cos((CENTER_LAT + (faces - half) * SPACING) * (math.pi / 180.0))

    plane = shape(ROWS, 128)
    pair = shape(2, ROWS, 128)
    both = call(
        pack_kernel, pair, (fields, diffusivity), "vv", limit=4 * 2**20, moved=400000
    )
    outward = pairs_over(sizes, lambda a, b: (a + 1 if b < 8 else a - 1, b))
    crossing = pairs_over(sizes, lambda a, b: (a - 1 if b < 8 else a + 1, b ^ 8))
    partner = swap_lon(both, 8)
    outer = lax.ppermute(both[1], ("lat", "lon"), outward)
    partner_outer = lax.ppermute(both[0], ("lat", "lon"), crossing)
    chunk = call(
        stencil_kernel,
        pair,
        (cosines, both, outer, partner, partner_outer),
        "svvvv",
        limit=4 * 2**20,
        moved=400000,
    )
    far = swap_lon(chunk, 7)
    near = [swap_lon(chunk, k) for k in (1, 2, 3)]
    far_near = [swap_lon(far, k) for k in (1, 2, 3)]
    first = call(
        first_weights_kernel,
        (shape(256, 3 * ROWS, dtype=BF16), shape(768, 256, dtype=BF16), shape(768, 256, dtype=BF16)),
        (w_embed, query_weight, key_weight, value_weight, far),
        "vvvvh",
        limit=8 * 2**20,
        moved=2000000,
    )
    *last, order = call(
        last_weights_kernel,
        (
            shape(2, 256, 256, dtype=BF16),
            shape(2, 256, 1024, dtype=BF16),
            shape(2, 1024, 256, dtype=BF16),
            shape(8, 128),
        ),
        (out_weight, up_weight, down_weight, chunk),
        "vvvh",
        limit=12 * 2**20,
        moved=5000000,
    )
    early = call(
        early_kernel,
        (
            shape(256, 256),
            shape(HEADS, 256, 112, dtype=BF16),
            shape(HEADS, 256, 128),
            plane,
            shape(16, 2, 128),
        ),
        (cosines, chunk, near[0], near[2], far, *first, order),
        "s" + 7 * "v" + "h",
        scratch=[pltpu.VMEM((HEADS, 112, 1024), BF16), pltpu.VMEM((HEADS, 80, 1024), BF16)],
        limit=40 * 2**20,
        flops=5 * 10**9,
        moved=3000000,
    )
    tile = shape(128, 256)
    send, *keys = call(
        late_kernel,
        (tile, shape(HEADS, 112, 1152, dtype=BF16), shape(HEADS, 80, 1152, dtype=BF16)),
        (cosines, near[1], *far_near, *first, *last, *early),
        "s" + 15 * "v",
        scratch=[pltpu.VMEM((16, 2, 128), F32), pltpu.VMEM((128, 128), F32)],
        limit=36 * 2**20,
        flops=5 * 10**9,
        moved=6000000,
    )
    own = call(
        own_kernel,
        tile,
        (*keys, *last, *early[:3]),
        8 * "v",
        limit=36 * 2**20,
        flops=3 * 10**9,
        moved=6000000,
    )
    received = swap_lon(send, 8)
    first = jnp.where(y == 0, own, received)
    second = jnp.where(y == 0, received, own)
    return jnp.stack([first, second])


def solution(mesh):
    placed = (P(None, "lat", "lon"), P("lat", "lon"), P(), P(), P(), P(), P(), P(), P())
    return jax.shard_map(
        on_device, mesh=mesh, in_specs=placed, out_specs=P("lat", "lon", None), check_vma=False
    )
```

```python
import functools
import math

import jax
import jax.numpy as jnp
from jax import lax
from jax.experimental import pallas as pl
from jax.experimental.pallas import tpu as pltpu
from jax.sharding import PartitionSpec as P

HEADS = 8
STEP_SIZE = 0.15
CENTER_LAT = 45.0
SPACING = 0.25
EPSILON = 1e-05
PARTNERS = (0, 1, 3, 7, 2, 6, 5, 4)
ROWS = 80
F32 = jnp.float32
BF16 = jnp.bfloat16
VMEM = pl.BlockSpec(memory_space=pltpu.VMEM)
SMEM = pl.BlockSpec(memory_space=pltpu.SMEM)


def split(values):
    high = values.astype(BF16)
    return high, (values - high.astype(F32)).astype(BF16)


def dot(left, right):
    return jnp.dot(left, right, preferred_element_type=F32)


def dot3(left, right):
    count = left[0].shape[0]
    sums = dot(jnp.concatenate(left, axis=0), right[0])
    return sums[:count] + sums[count:] + dot(left[0], right[1])


def pack_kernel(fields_ref, kappa_ref, both_ref):
    y = lax.axis_index("lon") // 8
    channels = fields_ref.shape[0]
    zero = jnp.zeros((1, 128), F32)
    rows = []
    for row in range(2):
        rows.append(
            jnp.concatenate([fields_ref[:, row, :], kappa_ref[row : row + 1, :], zero], axis=0)
        )
    flag = (jnp.zeros((ROWS, 128), jnp.int32) + y) == 0
    mine = jnp.where(flag, rows[0], rows[1])
    other = jnp.where(flag, rows[1], rows[0])
    both_ref[0] = mine
    both_ref[1] = other


def stencil_kernel(
    cos_ref, both_ref, outer_ref, partner_ref, partner_outer_ref, chunk_ref
):
    inverse = 1.0 / cos_ref[0]
    face_inner = cos_ref[1]
    face_outer = cos_ref[2]
    lane = lax.broadcasted_iota(jnp.int32, (ROWS, 128), 1)
    sectors = (
        (both_ref[0], both_ref[1], outer_ref[...]),
        (partner_ref[1], partner_ref[0], partner_outer_ref[...]),
    )
    for index, (q, inner, outer) in enumerate(sectors):
        kappa = q[78:79]
        lat_term = (0.5 * (kappa + inner[78:79]) * face_inner) * (inner - q)
        lat_term = lat_term + (0.5 * (kappa + outer[78:79]) * face_outer) * (outer - q)
        east = pltpu.roll(q, 127, 1)
        flux = (0.5 * (kappa + east[78:79])) * (east - q)
        flux = jnp.where(lane == 127, 0.0, flux)
        lon_term = flux - pltpu.roll(flux, 1, 1)
        updated = q + STEP_SIZE * ((lat_term + lon_term * inverse) * inverse)
        padded = jnp.concatenate([q, jnp.zeros((128 - ROWS, 128), F32)], axis=0)
        turned = jnp.transpose(padded)
        chunk_ref[index] = updated
        chunk_ref[index, 78:79, :] = turned[0:1]
        chunk_ref[index, 79:80, :] = turned[127:128]


def first_weights_kernel(*refs):
    sources = refs[:4]
    embed3_ref, qkv_high_ref, qkv_low_ref = refs[5:8]
    embed = jnp.concatenate([sources[0][...], jnp.zeros((128 - 78, 256), F32)], axis=0)
    high, low = split(jnp.transpose(embed)[:, :ROWS])
    embed3_ref[...] = jnp.concatenate([high, high, low], axis=1)
    for index in range(3):
        high, low = split(jnp.transpose(sources[1 + index][...]))
        qkv_high_ref[index * 256 : (index + 1) * 256, :] = high
        qkv_low_ref[index * 256 : (index + 1) * 256, :] = low


def last_weights_kernel(*refs):
    for source, target in zip(refs[:3], refs[4:7]):
        high, low = split(source[...])
        target[0] = high
        target[1] = low
    refs[7][...] = jnp.zeros_like(refs[7])


def layer_norm(values, axis):
    mean = jnp.mean(values, axis=axis, keepdims=True)
    centered = values - mean
    variance = jnp.mean(centered * centered, axis=axis, keepdims=True)
    return centered * lax.rsqrt(variance + EPSILON)


def embed_tokens(columns, embed3_ref):
    high, low = split(columns)
    hidden = dot(embed3_ref[...], jnp.concatenate([high, low, high], axis=0))
    return hidden, split(layer_norm(hidden, 0))


def store_keys(normed, masked, start, qkv_high_ref, qkv_low_ref, key3, value3):
    count = masked.shape[1]
    tokens = slice(start, start + count)
    high, low = split(dot3((qkv_high_ref[256:768, :], qkv_low_ref[256:768, :]), normed))
    row = lax.broadcasted_iota(jnp.int32, (16, count), 0)
    mask = jnp.where(jnp.logical_and(masked, row == 0), -1e30, 0.0).astype(BF16)
    ones = jnp.ones((16, count), BF16)
    for h in range(HEADS):
        rows = slice(32 * h, 32 * h + 32)
        key3[h, 0:32, tokens] = high[rows]
        key3[h, 32:64, tokens] = low[rows]
        key3[h, 64:96, tokens] = high[rows]
        key3[h, 96:112, tokens] = mask
        rows = slice(256 + 32 * h, 256 + 32 * h + 32)
        value3[h, 0:32, tokens] = high[rows]
        value3[h, 32:64, tokens] = low[rows]
        value3[h, 64:80, tokens] = ones


def face_fix(step, here, beyond):
    return step * (here[:, 78:79] + beyond[:, 78:79]) * (beyond - here)


def attend(queries, key3, value3, starts):
    nt = (((1,), (1,)), ((), ()))
    found = []
    scores = dot(queries(0), key3[0])
    for h in range(HEADS):
        later = dot(queries(h + 1), key3[h + 1]) if h + 1 < HEADS else None
        largest = jnp.max(scores, axis=1, keepdims=True)
        if starts is not None:
            largest = jnp.maximum(largest, starts(h))
        high, low = split(jnp.exp2(scores - largest))
        count = high.shape[0]
        sums = lax.dot_general(
            jnp.concatenate([high, low], axis=0), value3[h], nt, preferred_element_type=F32
        )
        sums = sums[:count] + sums[count:]
        found.append((largest, sums))
        scores = later
    return found


def place_edges(total, part, slot):
    lane = lax.broadcasted_iota(jnp.int32, (ROWS, 128), 1)
    total = jnp.where(lane == 2 * slot, pltpu.roll(part, 2 * slot, 1), total)
    return jnp.where(lane == 2 * slot + 1, pltpu.roll(part, 2 * slot + 2, 1), total)


def early_kernel(cos_ref, *refs):
    pieces = refs[:4]
    embed3_ref, qkv_high_ref, qkv_low_ref = refs[4:7]
    hidden_ref, query3_ref, state_ref, columns_ref, edges_ref = refs[8:13]
    key3, value3 = refs[13:]
    z = lax.axis_index("lon") % 8
    inverse = 1.0 / cos_ref[0]
    step = 0.5 * STEP_SIZE * inverse * inverse
    total = jnp.zeros((ROWS, 128), F32)
    for k in range(4):
        for index in range(2):
            edges_ref[2 * k + index] = pieces[k][index, 78:80, :]
            total = place_edges(total, pieces[k][index], 2 * k + index)
    columns_ref[...] = total
    wraps = jnp.logical_or(z == 0, z == 7).astype(jnp.int32)
    lane = lax.broadcasted_iota(jnp.int32, (ROWS, 128), 1)
    flag = (jnp.zeros((2, 128), jnp.int32) + z % 2) == 0
    outer = (jnp.zeros((2, 128), jnp.int32) + ((z + 1) // 2) % 2) == 0
    fixes = []
    for index in range(2):
        here = pieces[0][index, 78:80, :]
        beside = pieces[1][index, 78:80, :]
        wrapped = jnp.where(wraps == 1, 1 - index, index)
        across = jnp.where(outer, pieces[3][wrapped, 78:80, :], pieces[2][index, 78:80, :])
        west = jnp.where(flag, across, beside)
        east = jnp.where(flag, beside, across)
        fixes.append(face_fix(step, here[0:1], west[1:2]))
        fixes.append(face_fix(step, here[1:2], east[0:1]))
    fixes = jnp.transpose(jnp.concatenate(fixes + [jnp.zeros((124, 128), F32)], axis=0))[:ROWS]
    parts = []
    for index in range(2):
        part = pieces[0][index]
        part = part + jnp.where(lane == 0, fixes[:, 2 * index : 2 * index + 1], 0.0)
        part = part + jnp.where(lane == 127, fixes[:, 2 * index + 1 : 2 * index + 2], 0.0)
        parts.append(part)
    for k in range(1, 4):
        parts += [pieces[k][0], pieces[k][1]]
    hidden, normed = embed_tokens(jnp.concatenate(parts, axis=1), embed3_ref)
    hidden_ref[...] = jnp.transpose(hidden[:, :256])
    own = (normed[0][:, :256], normed[1][:, :256])
    scaled = dot3((qkv_high_ref[0:256], qkv_low_ref[0:256]), own)
    scaled = jnp.transpose(scaled * (math.log2(math.e) / math.sqrt(256 // HEADS)))
    high, low = split(scaled)
    row = lax.broadcasted_iota(jnp.int32, (256, 16), 1)
    mask = jnp.where(row == 0, 1.0, 0.0).astype(BF16)
    for h in range(HEADS):
        part = slice(32 * h, 32 * h + 32)
        query3_ref[h] = jnp.concatenate([high[:, part], high[:, part], low[:, part], mask], axis=1)
    lane = lax.broadcasted_iota(jnp.int32, (16, 1024), 1)
    edge = jnp.logical_or(lane % 128 == 0, lane % 128 == 127)
    store_keys(
        normed, jnp.logical_and(edge, lane >= 256), 0, qkv_high_ref, qkv_low_ref, key3, value3
    )
    found = attend(lambda h: query3_ref[h], key3, value3, None)
    for h, (largest, sums) in enumerate(found):
        state_ref[h] = jnp.concatenate([sums, jnp.broadcast_to(largest, (256, 48))], axis=1)


def finish(rows, key3, value3, out2_ref, up2_ref, down2_ref, hidden_ref, query3_ref, state_ref):
    found = attend(
        lambda h: query3_ref[h, rows, :], key3, value3, lambda h: state_ref[h, rows, 80:81]
    )
    attended = []
    for h, (largest, sums) in enumerate(found):
        before = state_ref[h, rows, :]
        sums = sums + before[:, 0:80] * jnp.exp2(before[:, 80:81] - largest)
        attended.append((sums[:, 0:32] + sums[:, 32:64]) / sums[:, 64:65])
    attended = split(jnp.concatenate(attended, axis=1))
    mixed = hidden_ref[rows, :] + dot3(attended, (out2_ref[0], out2_ref[1]))
    normed = split(layer_norm(mixed, 1))
    activated = split(jax.nn.gelu(dot3(normed, (up2_ref[0], up2_ref[1]))))
    return mixed + dot3(activated, (down2_ref[0], down2_ref[1]))


def own_kernel(*refs):
    refs[8][...] = finish(slice(0, 128), *refs[:8])


def late_kernel(cos_ref, *refs):
    pieces = refs[:4]
    embed3_ref, qkv_high_ref, qkv_low_ref, out2_ref, up2_ref, down2_ref = refs[4:10]
    hidden_ref, query3_ref, state_ref, columns_ref, edges_ref = refs[10:15]
    send_ref, key3, value3 = refs[15:18]
    edges, fixes = refs[18:]
    position = lax.axis_index("lon")
    y = position // 8
    z = position % 8
    inverse = 1.0 / cos_ref[0]
    step = 0.5 * STEP_SIZE * inverse * inverse
    total = columns_ref[...]
    for k in range(8):
        for index in range(2):
            half = y if index == 0 else 1 - y
            if k < 4:
                here = edges_ref[2 * k + index]
            else:
                here = pieces[k - 4][index, 78:80, :]
                total = place_edges(total, pieces[k - 4][index], 2 * k + index)
            edges[half * 8 + jnp.bitwise_xor(z, PARTNERS[k])] = here
    fixes[...] = jnp.zeros_like(fixes)
    for k in range(8):
        for index in range(2):
            half = y if index == 0 else 1 - y
            sector = half * 8 + jnp.bitwise_xor(z, PARTNERS[k])
            here = edges[sector]
            west = edges[(sector + 15) % 16]
            east = edges[(sector + 1) % 16]
            slot = 2 * (2 * k + index)
            fixes[slot : slot + 1, :] = face_fix(step, here[0:1], west[1:2])
            fixes[slot + 1 : slot + 2, :] = face_fix(step, here[1:2], east[0:1])
    total = total + jnp.transpose(fixes[...])[:ROWS]
    parts = [pieces[k][index] for k in range(4) for index in range(2)] + [total]
    hidden, normed = embed_tokens(jnp.concatenate(parts, axis=1), embed3_ref)
    lane = lax.broadcasted_iota(jnp.int32, (16, 1152), 1)
    edge = jnp.logical_or(lane % 128 == 0, lane % 128 == 127)
    unused = jnp.logical_or(lane < 1024 + 4, lane >= 1024 + 32)
    masked = jnp.where(lane < 1024, edge.astype(jnp.int32), unused.astype(jnp.int32)) == 1
    store_keys(normed, masked, 0, qkv_high_ref, qkv_low_ref, key3, value3)
    send_ref[...] = finish(
        slice(128, 256), key3, value3, out2_ref, up2_ref, down2_ref, hidden_ref, query3_ref, state_ref
    )


def shape(*dims, dtype=F32):
    return jax.ShapeDtypeStruct(dims, dtype)


def call(kernel, outs, operands, spaces, scratch=(), limit=None, flops=0, moved=0):
    kinds = {"s": SMEM, "v": VMEM, "h": pl.BlockSpec(memory_space=pltpu.HBM)}
    return pl.pallas_call(
        kernel,
        out_shape=outs,
        in_specs=[kinds[letter] for letter in spaces],
        out_specs=jax.tree.map(lambda _: VMEM, outs),
        scratch_shapes=scratch,
        compiler_params=pltpu.CompilerParams(vmem_limit_bytes=limit),
        cost_estimate=pl.CostEstimate(flops=flops, bytes_accessed=moved, transcendentals=0),
    )(*operands)


def pairs_over(axis_sizes, move):
    lats, lons = axis_sizes
    found = []
    for lat in range(lats):
        for lon in range(lons):
            target = move(lat, lon)
            if 0 <= target[0] < lats:
                found.append((lat * lons + lon, target[0] * lons + target[1]))
    return found


def swap_lon(values, mask):
    count = lax.axis_size("lon")
    return lax.ppermute(values, "lon", [(r, r ^ mask) for r in range(count)])


def on_device(
    fields, diffusivity, w_embed, query_weight, key_weight, value_weight, out_weight, up_weight, down_weight,
):
    sizes = (lax.axis_size("lat"), lax.axis_size("lon"))
    lat = lax.axis_index("lat")
    y = lax.axis_index("lon") // 8
    row = (2 * lat + y).astype(F32)
    faces = jnp.stack([row + 0.5, (2 * lat + 1).astype(F32), (2 * (lat + y)).astype(F32)])
    half = 0.5 * 2 * sizes[0]
    cosines = jnp.cos((CENTER_LAT + (faces - half) * SPACING) * (math.pi / 180.0))

    plane = shape(ROWS, 128)
    pair = shape(2, ROWS, 128)
    both = call(
        pack_kernel, pair, (fields, diffusivity), "vv", limit=4 * 2**20, moved=400000
    )
    outward = pairs_over(sizes, lambda a, b: (a + 1 if b < 8 else a - 1, b))
    crossing = pairs_over(sizes, lambda a, b: (a - 1 if b < 8 else a + 1, b ^ 8))
    partner = swap_lon(both, 8)
    outer = lax.ppermute(both[1], ("lat", "lon"), outward)
    partner_outer = lax.ppermute(both[0], ("lat", "lon"), crossing)
    chunk = call(
        stencil_kernel,
        pair,
        (cosines, both, outer, partner, partner_outer),
        "svvvv",
        limit=4 * 2**20,
        moved=400000,
    )
    far = swap_lon(chunk, 7)
    near = [swap_lon(chunk, k) for k in (1, 2, 3)]
    far_near = [swap_lon(far, k) for k in (1, 2, 3)]
    first = call(
        first_weights_kernel,
        (shape(256, 3 * ROWS, dtype=BF16), shape(768, 256, dtype=BF16), shape(768, 256, dtype=BF16)),
        (w_embed, query_weight, key_weight, value_weight, far),
        "vvvvh",
        limit=8 * 2**20,
        moved=2000000,
    )
    *last, order = call(
        last_weights_kernel,
        (
            shape(2, 256, 256, dtype=BF16),
            shape(2, 256, 1024, dtype=BF16),
            shape(2, 1024, 256, dtype=BF16),
            shape(8, 128),
        ),
        (out_weight, up_weight, down_weight, chunk),
        "vvvh",
        limit=12 * 2**20,
        moved=5000000,
    )
    early = call(
        early_kernel,
        (
            shape(256, 256),
            shape(HEADS, 256, 112, dtype=BF16),
            shape(HEADS, 256, 128),
            plane,
            shape(16, 2, 128),
        ),
        (cosines, chunk, near[0], near[2], far, *first, order),
        "s" + 7 * "v" + "h",
        scratch=[pltpu.VMEM((HEADS, 112, 1024), BF16), pltpu.VMEM((HEADS, 80, 1024), BF16)],
        limit=40 * 2**20,
        flops=5 * 10**9,
        moved=3000000,
    )
    tile = shape(128, 256)
    send, *keys = call(
        late_kernel,
        (tile, shape(HEADS, 112, 1152, dtype=BF16), shape(HEADS, 80, 1152, dtype=BF16)),
        (cosines, near[1], *far_near, *first, *last, *early),
        "s" + 15 * "v",
        scratch=[pltpu.VMEM((16, 2, 128), F32), pltpu.VMEM((128, 128), F32)],
        limit=36 * 2**20,
        flops=5 * 10**9,
        moved=6000000,
    )
    own = call(
        own_kernel,
        tile,
        (*keys, *last, *early[:3]),
        8 * "v",
        limit=36 * 2**20,
        flops=3 * 10**9,
        moved=6000000,
    )
    received = swap_lon(send, 8)
    first = jnp.where(y == 0, own, received)
    second = jnp.where(y == 0, received, own)
    return jnp.stack([first, second])


def solution(mesh):
    placed = (P(None, "lat", "lon"), P("lat", "lon"), P(), P(), P(), P(), P(), P(), P())
    return jax.shard_map(
        on_device, mesh=mesh, in_specs=placed, out_specs=P("lat", "lon", None), check_vma=False
    )
```

```python
import functools
import math

import jax
import jax.numpy as jnp
from jax import lax
from jax.experimental import pallas as pl
from jax.experimental.pallas import tpu as pltpu
from jax.sharding import PartitionSpec as P

HEADS = 8
STEP_SIZE = 0.15
CENTER_LAT = 45.0
SPACING = 0.25
EPSILON = 1e-05
PARTNERS = (0, 1, 3, 7, 2, 6, 5, 4)
ROWS = 80
F32 = jnp.float32
BF16 = jnp.bfloat16
VMEM = pl.BlockSpec(memory_space=pltpu.VMEM)
SMEM = pl.BlockSpec(memory_space=pltpu.SMEM)


def split(values):
    high = values.astype(BF16)
    return high, (values - high.astype(F32)).astype(BF16)


def dot(left, right):
    return jnp.dot(left, right, preferred_element_type=F32)


def dot3(left, right):
    count = left[0].shape[0]
    sums = dot(jnp.concatenate(left, axis=0), right[0])
    return sums[:count] + sums[count:] + dot(left[0], right[1])


def pack_kernel(fields_ref, kappa_ref, both_ref):
    y = lax.axis_index("lon") // 8
    channels = fields_ref.shape[0]
    zero = jnp.zeros((1, 128), F32)
    rows = []
    for row in range(2):
        rows.append(
            jnp.concatenate([fields_ref[:, row, :], kappa_ref[row : row + 1, :], zero], axis=0)
        )
    flag = (jnp.zeros((ROWS, 128), jnp.int32) + y) == 0
    mine = jnp.where(flag, rows[0], rows[1])
    other = jnp.where(flag, rows[1], rows[0])
    both_ref[0] = mine
    both_ref[1] = other


def stencil_kernel(
    cos_ref, both_ref, outer_ref, partner_ref, partner_outer_ref, chunk_ref
):
    inverse = 1.0 / cos_ref[0]
    face_inner = cos_ref[1]
    face_outer = cos_ref[2]
    lane = lax.broadcasted_iota(jnp.int32, (ROWS, 128), 1)
    sectors = (
        (both_ref[0], both_ref[1], outer_ref[...]),
        (partner_ref[1], partner_ref[0], partner_outer_ref[...]),
    )
    for index, (q, inner, outer) in enumerate(sectors):
        kappa = q[78:79]
        lat_term = (0.5 * (kappa + inner[78:79]) * face_inner) * (inner - q)
        lat_term = lat_term + (0.5 * (kappa + outer[78:79]) * face_outer) * (outer - q)
        east = pltpu.roll(q, 127, 1)
        flux = (0.5 * (kappa + east[78:79])) * (east - q)
        flux = jnp.where(lane == 127, 0.0, flux)
        lon_term = flux - pltpu.roll(flux, 1, 1)
        updated = q + STEP_SIZE * ((lat_term + lon_term * inverse) * inverse)
        padded = jnp.concatenate([q, jnp.zeros((128 - ROWS, 128), F32)], axis=0)
        turned = jnp.transpose(padded)
        chunk_ref[index] = updated
        chunk_ref[index, 78:79, :] = turned[0:1]
        chunk_ref[index, 79:80, :] = turned[127:128]


def first_weights_kernel(*refs):
    sources = refs[:4]
    embed3_ref, qkv_high_ref, qkv_low_ref = refs[5:8]
    embed = jnp.concatenate([sources[0][...], jnp.zeros((128 - 78, 256), F32)], axis=0)
    high, low = split(jnp.transpose(embed)[:, :ROWS])
    embed3_ref[...] = jnp.concatenate([high, high, low], axis=1)
    for index in range(3):
        high, low = split(jnp.transpose(sources[1 + index][...]))
        qkv_high_ref[index * 256 : (index + 1) * 256, :] = high
        qkv_low_ref[index * 256 : (index + 1) * 256, :] = low


def last_weights_kernel(*refs):
    for source, target in zip(refs[:3], refs[4:7]):
        high, low = split(source[...])
        target[0] = high
        target[1] = low


def layer_norm(values, axis):
    mean = jnp.mean(values, axis=axis, keepdims=True)
    centered = values - mean
    variance = jnp.mean(centered * centered, axis=axis, keepdims=True)
    return centered * lax.rsqrt(variance + EPSILON)


def embed_tokens(columns, embed3_ref):
    high, low = split(columns)
    hidden = dot(embed3_ref[...], jnp.concatenate([high, low, high], axis=0))
    return hidden, split(layer_norm(hidden, 0))


def store_keys(normed, masked, start, qkv_high_ref, qkv_low_ref, key3, value3):
    count = masked.shape[1]
    tokens = slice(start, start + count)
    high, low = split(dot3((qkv_high_ref[256:768, :], qkv_low_ref[256:768, :]), normed))
    row = lax.broadcasted_iota(jnp.int32, (16, count), 0)
    mask = jnp.where(jnp.logical_and(masked, row == 0), -1e30, 0.0).astype(BF16)
    ones = jnp.ones((16, count), BF16)
    for h in range(HEADS):
        rows = slice(32 * h, 32 * h + 32)
        key3[h, 0:32, tokens] = high[rows]
        key3[h, 32:64, tokens] = low[rows]
        key3[h, 64:96, tokens] = high[rows]
        key3[h, 96:112, tokens] = mask
        rows = slice(256 + 32 * h, 256 + 32 * h + 32)
        value3[h, 0:32, tokens] = high[rows]
        value3[h, 32:64, tokens] = low[rows]
        value3[h, 64:80, tokens] = ones


def face_fix(step, here, beyond):
    return step * (here[:, 78:79] + beyond[:, 78:79]) * (beyond - here)


def attend(queries, key3, value3, starts):
    nt = (((1,), (1,)), ((), ()))
    found = []
    scores = dot(queries(0), key3[0])
    for h in range(HEADS):
        later = dot(queries(h + 1), key3[h + 1]) if h + 1 < HEADS else None
        largest = jnp.max(scores, axis=1, keepdims=True)
        if starts is not None:
            largest = jnp.maximum(largest, starts(h))
        high, low = split(jnp.exp2(scores - largest))
        count = high.shape[0]
        sums = lax.dot_general(
            jnp.concatenate([high, low], axis=0), value3[h], nt, preferred_element_type=F32
        )
        sums = sums[:count] + sums[count:]
        found.append((largest, sums))
        scores = later
    return found


def place_edges(total, part, slot):
    lane = lax.broadcasted_iota(jnp.int32, (ROWS, 128), 1)
    total = jnp.where(lane == 2 * slot, pltpu.roll(part, 2 * slot, 1), total)
    return jnp.where(lane == 2 * slot + 1, pltpu.roll(part, 2 * slot + 2, 1), total)


def early_kernel(cos_ref, *refs):
    pieces = refs[:4]
    embed3_ref, qkv_high_ref, qkv_low_ref = refs[4:7]
    hidden_ref, query3_ref, state_ref, columns_ref, edges_ref = refs[7:12]
    key3, value3 = refs[12:]
    z = lax.axis_index("lon") % 8
    inverse = 1.0 / cos_ref[0]
    step = 0.5 * STEP_SIZE * inverse * inverse
    total = jnp.zeros((ROWS, 128), F32)
    for k in range(4):
        for index in range(2):
            edges_ref[2 * k + index] = pieces[k][index, 78:80, :]
            total = place_edges(total, pieces[k][index], 2 * k + index)
    columns_ref[...] = total
    wraps = jnp.logical_or(z == 0, z == 7).astype(jnp.int32)
    lane = lax.broadcasted_iota(jnp.int32, (ROWS, 128), 1)
    flag = (jnp.zeros((2, 128), jnp.int32) + z % 2) == 0
    outer = (jnp.zeros((2, 128), jnp.int32) + ((z + 1) // 2) % 2) == 0
    fixes = []
    for index in range(2):
        here = pieces[0][index, 78:80, :]
        beside = pieces[1][index, 78:80, :]
        wrapped = jnp.where(wraps == 1, 1 - index, index)
        across = jnp.where(outer, pieces[3][wrapped, 78:80, :], pieces[2][index, 78:80, :])
        west = jnp.where(flag, across, beside)
        east = jnp.where(flag, beside, across)
        fixes.append(face_fix(step, here[0:1], west[1:2]))
        fixes.append(face_fix(step, here[1:2], east[0:1]))
    fixes = jnp.transpose(jnp.concatenate(fixes + [jnp.zeros((124, 128), F32)], axis=0))[:ROWS]
    parts = []
    for index in range(2):
        part = pieces[0][index]
        part = part + jnp.where(lane == 0, fixes[:, 2 * index : 2 * index + 1], 0.0)
        part = part + jnp.where(lane == 127, fixes[:, 2 * index + 1 : 2 * index + 2], 0.0)
        parts.append(part)
    for k in range(1, 4):
        parts += [pieces[k][0], pieces[k][1]]
    hidden, normed = embed_tokens(jnp.concatenate(parts, axis=1), embed3_ref)
    hidden_ref[...] = jnp.transpose(hidden[:, :256])
    own = (normed[0][:, :256], normed[1][:, :256])
    scaled = dot3((qkv_high_ref[0:256], qkv_low_ref[0:256]), own)
    scaled = jnp.transpose(scaled * (math.log2(math.e) / math.sqrt(256 // HEADS)))
    high, low = split(scaled)
    row = lax.broadcasted_iota(jnp.int32, (256, 16), 1)
    mask = jnp.where(row == 0, 1.0, 0.0).astype(BF16)
    for h in range(HEADS):
        part = slice(32 * h, 32 * h + 32)
        query3_ref[h] = jnp.concatenate([high[:, part], high[:, part], low[:, part], mask], axis=1)
    lane = lax.broadcasted_iota(jnp.int32, (16, 1024), 1)
    edge = jnp.logical_or(lane % 128 == 0, lane % 128 == 127)
    store_keys(
        normed, jnp.logical_and(edge, lane >= 256), 0, qkv_high_ref, qkv_low_ref, key3, value3
    )
    found = attend(lambda h: query3_ref[h], key3, value3, None)
    for h, (largest, sums) in enumerate(found):
        state_ref[h] = jnp.concatenate([sums, jnp.broadcast_to(largest, (256, 48))], axis=1)


def finish(rows, key3, value3, out2_ref, up2_ref, down2_ref, hidden_ref, query3_ref, state_ref):
    found = attend(
        lambda h: query3_ref[h, rows, :], key3, value3, lambda h: state_ref[h, rows, 80:81]
    )
    attended = []
    for h, (largest, sums) in enumerate(found):
        before = state_ref[h, rows, :]
        sums = sums + before[:, 0:80] * jnp.exp2(before[:, 80:81] - largest)
        attended.append((sums[:, 0:32] + sums[:, 32:64]) / sums[:, 64:65])
    attended = split(jnp.concatenate(attended, axis=1))
    mixed = hidden_ref[rows, :] + dot3(attended, (out2_ref[0], out2_ref[1]))
    normed = split(layer_norm(mixed, 1))
    activated = split(jax.nn.gelu(dot3(normed, (up2_ref[0], up2_ref[1]))))
    return mixed + dot3(activated, (down2_ref[0], down2_ref[1]))


def own_kernel(*refs):
    refs[8][...] = finish(slice(0, 128), *refs[:8])


def late_kernel(cos_ref, *refs):
    pieces = refs[:4]
    embed3_ref, qkv_high_ref, qkv_low_ref, out2_ref, up2_ref, down2_ref = refs[4:10]
    hidden_ref, query3_ref, state_ref, columns_ref, edges_ref = refs[10:15]
    send_ref, key3, value3 = refs[15:18]
    edges, fixes = refs[18:]
    position = lax.axis_index("lon")
    y = position // 8
    z = position % 8
    inverse = 1.0 / cos_ref[0]
    step = 0.5 * STEP_SIZE * inverse * inverse
    total = columns_ref[...]
    for k in range(8):
        for index in range(2):
            half = y if index == 0 else 1 - y
            if k < 4:
                here = edges_ref[2 * k + index]
            else:
                here = pieces[k - 4][index, 78:80, :]
                total = place_edges(total, pieces[k - 4][index], 2 * k + index)
            edges[half * 8 + jnp.bitwise_xor(z, PARTNERS[k])] = here
    fixes[...] = jnp.zeros_like(fixes)
    for k in range(8):
        for index in range(2):
            half = y if index == 0 else 1 - y
            sector = half * 8 + jnp.bitwise_xor(z, PARTNERS[k])
            here = edges[sector]
            west = edges[(sector + 15) % 16]
            east = edges[(sector + 1) % 16]
            slot = 2 * (2 * k + index)
            fixes[slot : slot + 1, :] = face_fix(step, here[0:1], west[1:2])
            fixes[slot + 1 : slot + 2, :] = face_fix(step, here[1:2], east[0:1])
    total = total + jnp.transpose(fixes[...])[:ROWS]
    parts = [pieces[k][index] for k in range(4) for index in range(2)] + [total]
    hidden, normed = embed_tokens(jnp.concatenate(parts, axis=1), embed3_ref)
    lane = lax.broadcasted_iota(jnp.int32, (16, 1152), 1)
    edge = jnp.logical_or(lane % 128 == 0, lane % 128 == 127)
    unused = jnp.logical_or(lane < 1024 + 4, lane >= 1024 + 32)
    masked = jnp.where(lane < 1024, edge.astype(jnp.int32), unused.astype(jnp.int32)) == 1
    store_keys(normed, masked, 0, qkv_high_ref, qkv_low_ref, key3, value3)
    send_ref[...] = finish(
        slice(128, 256), key3, value3, out2_ref, up2_ref, down2_ref, hidden_ref, query3_ref, state_ref
    )


def shape(*dims, dtype=F32):
    return jax.ShapeDtypeStruct(dims, dtype)


def call(kernel, outs, operands, spaces, scratch=(), limit=None, flops=0, moved=0):
    kinds = {"s": SMEM, "v": VMEM, "h": pl.BlockSpec(memory_space=pltpu.HBM)}
    return pl.pallas_call(
        kernel,
        out_shape=outs,
        in_specs=[kinds[letter] for letter in spaces],
        out_specs=jax.tree.map(lambda _: VMEM, outs),
        scratch_shapes=scratch,
        compiler_params=pltpu.CompilerParams(vmem_limit_bytes=limit),
        cost_estimate=pl.CostEstimate(flops=flops, bytes_accessed=moved, transcendentals=0),
    )(*operands)


def pairs_over(axis_sizes, move):
    lats, lons = axis_sizes
    found = []
    for lat in range(lats):
        for lon in range(lons):
            target = move(lat, lon)
            if 0 <= target[0] < lats:
                found.append((lat * lons + lon, target[0] * lons + target[1]))
    return found


def swap_lon(values, mask):
    count = lax.axis_size("lon")
    return lax.ppermute(values, "lon", [(r, r ^ mask) for r in range(count)])


def on_device(
    fields, diffusivity, w_embed, query_weight, key_weight, value_weight, out_weight, up_weight, down_weight,
):
    sizes = (lax.axis_size("lat"), lax.axis_size("lon"))
    lat = lax.axis_index("lat")
    y = lax.axis_index("lon") // 8
    row = (2 * lat + y).astype(F32)
    faces = jnp.stack([row + 0.5, (2 * lat + 1).astype(F32), (2 * (lat + y)).astype(F32)])
    half = 0.5 * 2 * sizes[0]
    cosines = jnp.cos((CENTER_LAT + (faces - half) * SPACING) * (math.pi / 180.0))

    plane = shape(ROWS, 128)
    pair = shape(2, ROWS, 128)
    both = call(
        pack_kernel, pair, (fields, diffusivity), "vv", limit=4 * 2**20, moved=400000
    )
    outward = pairs_over(sizes, lambda a, b: (a + 1 if b < 8 else a - 1, b))
    crossing = pairs_over(sizes, lambda a, b: (a - 1 if b < 8 else a + 1, b ^ 8))
    partner = swap_lon(both, 8)
    outer = lax.ppermute(both[1], ("lat", "lon"), outward)
    partner_outer = lax.ppermute(both[0], ("lat", "lon"), crossing)
    chunk = call(
        stencil_kernel,
        pair,
        (cosines, both, outer, partner, partner_outer),
        "svvvv",
        limit=4 * 2**20,
        moved=400000,
    )
    far = swap_lon(chunk, 7)
    near = [swap_lon(chunk, k) for k in (1, 2, 3)]
    far_near = [swap_lon(far, k) for k in (1, 2, 3)]
    first = call(
        first_weights_kernel,
        (shape(256, 3 * ROWS, dtype=BF16), shape(768, 256, dtype=BF16), shape(768, 256, dtype=BF16)),
        (w_embed, query_weight, key_weight, value_weight, both),
        "vvvvh",
        limit=8 * 2**20,
        moved=2000000,
    )
    early = call(
        early_kernel,
        (
            shape(256, 256),
            shape(HEADS, 256, 112, dtype=BF16),
            shape(HEADS, 256, 128),
            plane,
            shape(16, 2, 128),
        ),
        (cosines, chunk, near[0], near[2], far, *first),
        "s" + 7 * "v",
        scratch=[pltpu.VMEM((HEADS, 112, 1024), BF16), pltpu.VMEM((HEADS, 80, 1024), BF16)],
        limit=40 * 2**20,
        flops=5 * 10**9,
        moved=3000000,
    )
    last = call(
        last_weights_kernel,
        (
            shape(2, 256, 256, dtype=BF16),
            shape(2, 256, 1024, dtype=BF16),
            shape(2, 1024, 256, dtype=BF16),
        ),
        (out_weight, up_weight, down_weight, early[3]),
        "vvvh",
        limit=12 * 2**20,
        moved=5000000,
    )
    tile = shape(128, 256)
    send, *keys = call(
        late_kernel,
        (tile, shape(HEADS, 112, 1152, dtype=BF16), shape(HEADS, 80, 1152, dtype=BF16)),
        (cosines, near[1], *far_near, *first, *last, *early),
        "s" + 15 * "v",
        scratch=[pltpu.VMEM((16, 2, 128), F32), pltpu.VMEM((128, 128), F32)],
        limit=36 * 2**20,
        flops=5 * 10**9,
        moved=6000000,
    )
    own = call(
        own_kernel,
        tile,
        (*keys, *last, *early[:3]),
        8 * "v",
        limit=36 * 2**20,
        flops=3 * 10**9,
        moved=6000000,
    )
    received = swap_lon(send, 8)
    first = jnp.where(y == 0, own, received)
    second = jnp.where(y == 0, received, own)
    return jnp.stack([first, second])


def solution(mesh):
    placed = (P(None, "lat", "lon"), P("lat", "lon"), P(), P(), P(), P(), P(), P(), P())
    return jax.shard_map(
        on_device, mesh=mesh, in_specs=placed, out_specs=P("lat", "lon", None), check_vma=False
    )
```
